512 devices in a mesh: dp: 64 (over x_hi, z, core), mp: 8 (over x_lo, y).
Axes of the slice: x: 4 (x_hi: 2, x_lo: 2; x = x_hi * 2 + x_lo), y: 4, z: 16, core: 2. Of those that a mesh axis runs over, the one named last changes fastest.
Arguments:
- tokens: bfloat16 [16384, 6144], P('dp', 'mp'), may hold values from -6 to 6
- w_in: bfloat16 [128, 48, 512], P('dp', 'mp'), may hold values from -0.5 to 0.5
- w_out: bfloat16 [512, 48, 128], P('dp', 'mp'), may hold values from -0.25 to 0.25
- cotangent: bfloat16 [16384, 6144], P('dp', 'mp'), may hold values from -6 to 6
Outputs:
- output: bfloat16 [16384, 6144], P('dp', 'mp')
- grad_tokens: bfloat16 [16384, 6144], P('dp', 'mp')
- grad_in: float32 [128, 48, 512], P('dp', 'mp')
- grad_out: float32 [512, 48, 128], P('dp', 'mp')
The draws below stay inside these ranges and needn't reach their ends.
All inputs are finite; a program needn't handle non-finite values.
Results may differ from the reference program's by a relative error of at most 0.0057.
Values may be sent and summed in bfloat16 or wider, within the bound.
No kernel may reach another device: no remote copies, remote signals or barrier semaphores. Data moves between devices by JAX's collectives and lax.ppermute only.
A program may use at most 64 MiB of HBM per device.

```python
import jax
import jax.numpy as jnp
from jax import lax

D = 6144
BLK = 128
NB = 48
EXP = 512
TILES = 192
TOK_DEV = 256
TOKENS = 16384
N_DP = 64


def block_levels(rng, dims, cuts, smallest, top_value):
    def one(dim, parts):
        draws = jax.random.uniform(jax.random.fold_in(jax.random.fold_in(rng, 6), dim), (parts,), jnp.float32, smallest / len(cuts), top_value / len(cuts))
        return jnp.repeat(jnp.exp(draws), dims[dim] // parts).reshape((-1,) + (1,) * (len(dims) - dim - 1))

    loudness = one(*cuts[0])
    for cut in cuts[1:]:
        loudness = loudness * one(*cut)
    return loudness


def scatter_about(key, extent, width, reach, split=(), held_as=jnp.bfloat16):
    result = width * jax.random.normal(key, extent, jnp.float32)
    if split:
        result = result * block_levels(key, extent, split, -0.22, 0.18)
    return jnp.clip(result, -reach, reach).astype(held_as)


def setup_inputs(seed: int = 0) -> dict:
    key_list = jax.random.split(jax.random.key(seed), 5)
    tokens = scatter_about(key_list[0], (TOKENS, D), 1.0, 6.0, ((0, 64), (1, 8)))
    w_in = scatter_about(key_list[1], (BLK, NB, EXP), BLK ** -0.5, 0.5, ((0, 64), (1, 8)))
    w_out = scatter_about(key_list[2], (EXP, NB, BLK), EXP ** -0.5, 0.25, ((0, 64), (1, 8)))
    cotangent = scatter_about(key_list[3], (TOKENS, D), 1.0, 6.0, ((0, 64), (1, 8)))
    return {"tokens": tokens, "w_in": w_in, "w_out": w_out, "cotangent": cotangent}


def gelu_tanh(value):
    return jax.nn.gelu(value, approximate=True)

def reference(tokens, w_in, w_out, cotangent):
    f32 = jnp.float32
    win_f = w_in.astype(f32)
    wout_f = w_out.astype(f32)
    xs = tokens.reshape(N_DP, TOK_DEV, D)
    cs = cotangent.reshape(N_DP, TOK_DEV, D)

    def step(carry, pair):
        acc_in, acc_out = carry
        xblock, cblock = pair
        x3 = xblock.reshape(TOK_DEV, NB, BLK).astype(f32)
        pre = jnp.einsum('tir,rie->tie', x3, win_f)
        act = gelu_tanh(pre).astype(jnp.bfloat16)
        mixed = act.reshape(TOK_DEV, TILES, BLK).transpose(0, 2, 1).reshape(TOK_DEV, NB, EXP)
        mixed_f = mixed.astype(f32)
        out = jnp.einsum('toe,eon->ton', mixed_f, wout_f).astype(jnp.bfloat16).reshape(TOK_DEV, D)
        c3 = cblock.reshape(TOK_DEV, NB, BLK).astype(f32)
        d_mixed = jnp.einsum('ton,eon->toe', c3, wout_f).astype(jnp.bfloat16)
        acc_out = acc_out + jnp.einsum('toe,ton->eon', mixed_f, c3)
        d_act = d_mixed.reshape(TOK_DEV, BLK, TILES).transpose(0, 2, 1).reshape(TOK_DEV, NB, EXP)
        _, pull = jax.vjp(gelu_tanh, pre)
        d_pre = pull(d_act.astype(f32))[0].astype(jnp.bfloat16)
        d_pre_f = d_pre.astype(f32)
        grad_x = jnp.einsum('tie,rie->tir', d_pre_f, win_f).astype(jnp.bfloat16).reshape(TOK_DEV, D)
        acc_in = acc_in + jnp.einsum('tir,tie->rie', x3, d_pre_f)
        return ((acc_in, acc_out), (out, grad_x))
    start = (jnp.zeros((BLK, NB, EXP), f32), jnp.zeros((EXP, NB, BLK), f32))
    (acc_in, acc_out), (outs, grads) = lax.scan(step, start, (xs, cs))
    scale = f32(1.0) / jnp.sqrt(f32(TOKENS))
    output = outs.reshape(TOKENS, D)
    grad_tokens = grads.reshape(TOKENS, D)
    return (output, grad_tokens, acc_in * scale, acc_out * scale)
```

```python
import jax
import jax.numpy as jnp
from jax import lax
from jax.sharding import Mesh, PartitionSpec as P

BLK = 128
NB = 48
EXP = 512
TILES = 192

DP = ("x_hi", "z_hi", "z_lo", "core")
MP = ("x_lo", "y")
SIZES = (2, 4, 4, 2, 2, 4)


def gelu_tanh(value):
    return jax.nn.gelu(value, approximate=True)


def exchange(value, axis):
    return lax.all_to_all(value, axis, 0, 0, tiled=True)


def gather_weights(w_in, w_out):
    shard = jnp.concatenate(
        [w_in.transpose(1, 0, 2).reshape(48, 128), w_out.transpose(1, 0, 2).reshape(48, 128)]
    )
    along_z = lax.all_gather(shard, ("z_hi", "z_lo"), axis=0, tiled=False)
    halves = lax.all_gather(along_z, "x_hi", axis=0, tiled=False)
    full = lax.all_gather(halves, "core", axis=0, tiled=False)
    full = full.transpose(1, 2, 0, 3, 4).reshape(64, 96, 128)
    win = full[:, :48].reshape(64, 6, 2, 512).transpose(1, 0, 2, 3).reshape(6, 128, 512)
    wout = full[:, 48:].reshape(64, 6, 8, 128).transpose(1, 0, 2, 3).reshape(6, 512, 128)
    return win, wout


def scatter_sums(part_in, part_out):
    f32 = jnp.float32
    bf16 = jnp.bfloat16
    rows_in = part_in.reshape(6, 64, 2, 512).transpose(1, 0, 2, 3).reshape(64, 48, 128)
    rows_out = part_out.reshape(6, 64, 8, 128).transpose(1, 0, 2, 3).reshape(64, 48, 128)
    both = jnp.concatenate([rows_in, rows_out], axis=1).astype(bf16)
    both = both.reshape(2, 4, 4, 2, 96, 128).transpose(3, 0, 2, 1, 4, 5)
    got = exchange(both, "core")
    both = got.astype(f32).sum(axis=0).astype(bf16).reshape(8, 4, 96, 128)
    got = exchange(both, ("x_hi", "z_lo"))
    both = got.astype(f32).sum(axis=0).astype(bf16)
    got = exchange(both, "z_hi")
    total = got.astype(f32).sum(axis=0)
    grad_in = total[:48].reshape(6, 2, 512).transpose(1, 0, 2)
    grad_out = total[48:].reshape(6, 8, 128).transpose(1, 0, 2)
    return grad_in, grad_out


def on_device(tokens, w_in, w_out, cotangent):
    f32 = jnp.float32
    bf16 = jnp.bfloat16
    rows = tokens.shape[0]
    groups = 8
    nb_local = NB // groups
    tiles_local = nb_local * EXP // BLK
    piece_cols = BLK // groups
    x3 = tokens.reshape(rows, nb_local, BLK)
    c3 = cotangent.reshape(rows, nb_local, BLK)
    scale = 1.0 / jnp.sqrt(f32(rows * 64))
    win, wout = gather_weights(w_in, w_out)
    pre = jnp.einsum("tir,ire->tie", x3, win, preferred_element_type=f32)
    act = gelu_tanh(pre).astype(bf16)
    tiled = act.reshape(rows, tiles_local, BLK)
    moved = lax.all_to_all(tiled, MP, split_axis=2, concat_axis=1, tiled=True)
    mixed_part = moved.transpose(0, 2, 1).reshape(rows, nb_local, EXP)
    out_part = jnp.einsum("toe,oen->ton", mixed_part, wout, preferred_element_type=f32)
    output = out_part.astype(bf16).reshape(rows, nb_local * BLK)
    d_mixed = jnp.einsum("ton,oen->toe", c3, wout, preferred_element_type=f32).astype(bf16)
    part_out = jnp.einsum("toe,ton->oen", mixed_part, c3, preferred_element_type=f32)
    back_send = d_mixed.reshape(rows, piece_cols, TILES).transpose(0, 2, 1)
    back = lax.all_to_all(back_send, MP, split_axis=1, concat_axis=2, tiled=True)
    d_act = back.reshape(rows, nb_local, EXP)
    _, pull = jax.vjp(gelu_tanh, pre)
    d_pre = pull(d_act.astype(f32))[0].astype(bf16)
    grad_x = jnp.einsum("tie,ire->tir", d_pre, win, preferred_element_type=f32)
    grad_tokens = grad_x.astype(bf16).reshape(rows, nb_local * BLK)
    part_in = jnp.einsum("tir,tie->ire", x3, d_pre, preferred_element_type=f32)
    grad_in, grad_out = scatter_sums(part_in * scale, part_out * scale)
    return (output, grad_tokens, grad_in, grad_out)


def solution(mesh):
    fine = Mesh(mesh.devices.reshape(SIZES), DP + MP)
    placed = (P(DP, MP), P(DP, MP, None), P(DP, MP, None), P(DP, MP))
    return jax.shard_map(
        on_device,
        mesh=fine,
        in_specs=placed,
        out_specs=(P(DP, MP), P(DP, MP), P(DP, MP, None), P(DP, MP, None)),
        check_vma=False,
    )
```

```python
import jax
import jax.numpy as jnp
from jax import lax
from jax.sharding import Mesh, PartitionSpec as P

BLK = 128
NB = 48
EXP = 512
TILES = 192

DP = ("x_hi", "z_hi", "z_lo", "core")
MP = ("x_lo", "y")
SIZES = (2, 4, 4, 2, 2, 4)


def gelu_tanh(value):
    return jax.nn.gelu(value, approximate=True)


def exchange(value, axis):
    return lax.all_to_all(value, axis, 0, 0, tiled=True)


def gather_weights(w_in, w_out):
    shard = jnp.concatenate(
        [w_in.transpose(1, 0, 2).reshape(48, 128), w_out.transpose(1, 0, 2).reshape(48, 128)]
    )
    along_z = lax.all_gather(shard, ("z_hi", "z_lo"), axis=0, tiled=False)
    halves = lax.all_gather(along_z, "x_hi", axis=0, tiled=False).reshape(1, 32, 96, 128)
    full = exchange(jnp.broadcast_to(halves, (2, 32, 96, 128)), "core")
    full = full.transpose(1, 0, 2, 3).reshape(64, 96, 128)
    win = full[:, :48].reshape(64, 6, 2, 512).transpose(1, 0, 2, 3).reshape(6, 128, 512)
    wout = full[:, 48:].reshape(64, 6, 8, 128).transpose(1, 0, 2, 3).reshape(6, 512, 128)
    return win, wout


def half_sum(part, keep):
    cols = part.shape[2]
    both = part.astype(jnp.bfloat16).reshape(6, 2, 4, 4, 2, keep, cols)
    both = both.transpose(4, 1, 3, 2, 0, 5, 6).reshape(2, 32, 48, 128)
    got = exchange(both, "core")
    return got.astype(jnp.float32).sum(axis=0).astype(jnp.bfloat16)


def scatter_sums(half_in, half_out):
    f32 = jnp.float32
    both = jnp.concatenate([half_in, half_out], axis=1).reshape(8, 4, 96, 128)
    got = exchange(both, ("x_hi", "z_lo"))
    both = got.astype(f32).sum(axis=0).astype(jnp.bfloat16)
    got = exchange(both, "z_hi")
    total = got.astype(f32).sum(axis=0)
    grad_in = total[:48].reshape(6, 2, 512).transpose(1, 0, 2)
    grad_out = total[48:].reshape(6, 8, 128).transpose(1, 0, 2)
    return grad_in, grad_out


def on_device(tokens, w_in, w_out, cotangent):
    f32 = jnp.float32
    bf16 = jnp.bfloat16
    rows = tokens.shape[0]
    groups = 8
    nb_local = NB // groups
    tiles_local = nb_local * EXP // BLK
    piece_cols = BLK // groups
    x3 = tokens.reshape(rows, nb_local, BLK)
    c3 = cotangent.reshape(rows, nb_local, BLK)
    scale = 1.0 / jnp.sqrt(f32(rows * 64))
    win, wout = gather_weights(w_in, w_out)
    d_mixed = jnp.einsum("ton,oen->toe", c3, wout, preferred_element_type=f32).astype(bf16)
    back_send = d_mixed.reshape(rows, piece_cols, TILES).transpose(0, 2, 1)
    back = lax.all_to_all(back_send, MP, split_axis=1, concat_axis=2, tiled=True)
    pre = jnp.einsum("tir,ire->tie", x3, win, preferred_element_type=f32)
    act = gelu_tanh(pre).astype(bf16)
    act, pre = lax.optimization_barrier((act, pre))
    tiled = act.reshape(rows, tiles_local, BLK)
    moved = lax.all_to_all(tiled, MP, split_axis=2, concat_axis=1, tiled=True)
    d_act = back.reshape(rows, nb_local, EXP)
    _, pull = jax.vjp(gelu_tanh, pre)
    d_pre = pull(d_act.astype(f32))[0].astype(bf16)
    part_in = jnp.einsum("tir,tie->ire", x3, d_pre, preferred_element_type=f32)
    half_in = half_sum(part_in * scale, 2)
    mixed_part = moved.transpose(0, 2, 1).reshape(rows, nb_local, EXP)
    part_out = jnp.einsum("toe,ton->oen", mixed_part, c3, preferred_element_type=f32)
    half_out = half_sum(part_out * scale, 8)
    grad_in, grad_out = scatter_sums(half_in, half_out)
    grad_x = jnp.einsum("tie,ire->tir", d_pre, win, preferred_element_type=f32)
    grad_tokens = grad_x.astype(bf16).reshape(rows, nb_local * BLK)
    out_part = jnp.einsum("toe,oen->ton", mixed_part, wout, preferred_element_type=f32)
    output = out_part.astype(bf16).reshape(rows, nb_local * BLK)
    return (output, grad_tokens, grad_in, grad_out)


def solution(mesh):
    fine = Mesh(mesh.devices.reshape(SIZES), DP + MP)
    placed = (P(DP, MP), P(DP, MP, None), P(DP, MP, None), P(DP, MP))
    return jax.shard_map(
        on_device,
        mesh=fine,
        in_specs=placed,
        out_specs=(P(DP, MP), P(DP, MP), P(DP, MP, None), P(DP, MP, None)),
        check_vma=False,
    )
```

```python
import jax
import jax.numpy as jnp
from jax import lax
from jax.experimental import pallas as pl
from jax.experimental.pallas import tpu as pltpu
from jax.sharding import Mesh, PartitionSpec as P

NB = 6
ROWS = 256
DP = ("x_hi", "z_hi", "z_lo", "core")
MP = ("x_lo", "y")
SIZES = (2, 4, 4, 2, 2, 4)
F32 = jnp.float32
BF16 = jnp.bfloat16
PARAMS = pltpu.CompilerParams(vmem_limit_bytes=40 * 1024 * 1024)
SMEM = pl.BlockSpec(memory_space=pltpu.SMEM)
VMEM = pl.BlockSpec(memory_space=pltpu.VMEM)


def dot(lhs, rhs, lhs_dim, rhs_dim):
    return lax.dot_general(
        lhs, rhs, (((lhs_dim,), (rhs_dim,)), ((), ())), preferred_element_type=F32
    )


def halves(value, step):
    return value[:, step * 128 : (step + 1) * 128]


def back_kernel(at_ref, mine_ref, other_ref, c_ref, send_ref, wout_ref, left, right):
    first = at_ref[1] == 0
    for pair in range(NB // 2):
        rows = slice(48 + pair * 16, 48 + pair * 16 + 16)
        mine = mine_ref[:, rows, :].astype(F32)
        other = other_ref[:, rows, :].astype(F32)
        zero = jnp.where(first, mine, other)
        one = jnp.where(first, other, mine)
        for k in range(2):
            o = pair * 2 + k
            cut = slice(k * 8, k * 8 + 8)
            wide = jnp.stack([zero[:, cut], one[:, cut]], axis=1).reshape(512, 128)
            w = wide.astype(BF16)
            wout_ref[o] = w
            d = dot(w, c_ref[:, o * 128 : (o + 1) * 128], 1, 1)
            left[o * 512 : (o + 1) * 512, :] = d[:, :128]
            right[o * 512 : (o + 1) * 512, :] = d[:, 128:]
    for p in range(8):
        for g in range(24):
            at = pl.ds(p * 24 + g, 16, stride=192)
            send_ref[p, g, :, :128] = left[at, :].astype(BF16)
            send_ref[p, g, :, 128:] = right[at, :].astype(BF16)


def forward_kernel(at_ref, mine_ref, other_ref, x_ref, *rest):
    sends, (slope_ref, win_ref, mine_f, other_f, w_f, act) = rest[:8], rest[8:]
    place, first = at_ref[0], at_ref[1] == 0
    mine_f[...] = mine_ref[:, :48, :].astype(F32).reshape(32 * 48, 128)
    other_f[...] = other_ref[:, :48, :].astype(F32).reshape(32 * 48, 128)
    root = 0.7978845608028654
    for i in range(NB):
        for k in range(2):
            for c in range(4):
                at = pl.ds(i * 8 + k * 4 + c, 32, stride=48)
                mine, other = mine_f[at, :], other_f[at, :]
                w_f[c, pl.ds(k, 32, stride=4), :] = jnp.where(first, mine, other)
                w_f[c, pl.ds(2 + k, 32, stride=4), :] = jnp.where(first, other, mine)
        for c in range(4):
            w = w_f[c].astype(BF16)
            win_ref[i, :, c * 128 : (c + 1) * 128] = w
            v = dot(w, x_ref[:, i * 128 : (i + 1) * 128], 0, 1)
            square = v * v
            th = jnp.tanh(root * (v + 0.044715 * (v * square)))
            half = 0.5 * (1.0 + th)
            act[i * 4 + c] = (v * half).astype(BF16).reshape(8, 16, ROWS)
            slope_ref[i, c * 128 : (c + 1) * 128, :] = half + (0.5 * root) * v * (
                1.0 - th * th
            ) * (1.0 + 0.134145 * square)
    for s in range(8):
        to = lax.rem(place + s, 8)
        sends[s][...] = act[:, to]


def store_ordered(ref, rows, value):
    for n in range(32):
        ref[n // 16 * 16 + n % 4 * 4 + n // 4 % 4, rows, :] = value[n]


def first_grad_kernel(at_ref, back_ref, slope_ref, x_ref, dpre_ref, keep_ref, send_ref, p_f, o_f):
    first = at_ref[1] == 0
    for i in range(NB):
        parts = [back_ref[:, i * 4 + a].reshape(128, ROWS) for a in range(4)]
        x = x_ref[:, i * 128 : (i + 1) * 128]
        for c in range(4):
            d = (parts[c].astype(F32) * slope_ref[i, c * 128 : (c + 1) * 128, :]).astype(BF16)
            dpre_ref[i, c * 128 : (c + 1) * 128, :] = d
            p_f[c] = dot(x, d, 0, 1)
            for core in range(2):
                for k in range(2):
                    o_f[core, pl.ds(i * 8 + k * 4 + c, 32, stride=48), :] = p_f[
                        c, pl.ds(core * 2 + k, 32, stride=4), :
                    ]
    zero = o_f[0].reshape(32, 48, 128)
    one = o_f[1].reshape(32, 48, 128)
    store_ordered(keep_ref, slice(0, 48), jnp.where(first, zero, one).astype(BF16))
    store_ordered(send_ref, slice(0, 48), jnp.where(first, one, zero).astype(BF16))


def second_grad_kernel(at_ref, *rest):
    pieces, (c_ref, mixed_ref, keep_ref, send_ref, left, right) = rest[:8], rest[8:]
    place, first = at_ref[0], at_ref[1] == 0
    for s in range(8):
        start = pl.multiple_of(lax.rem(place + 8 - s, 8) * 384, 384)
        piece = pieces[s][...].reshape(384, ROWS).astype(F32)
        left[pl.ds(start, 384), :] = piece[:, :128]
        right[pl.ds(start, 384), :] = piece[:, 128:]
    for j in range(16):
        at = pl.ds(j, 192, stride=16)
        mixed_ref[j * 192 : (j + 1) * 192, :128] = left[at, :].astype(BF16)
        mixed_ref[j * 192 : (j + 1) * 192, 128:] = right[at, :].astype(BF16)
    for pair in range(NB // 2):
        kept, sent = [], []
        for k in range(2):
            o = pair * 2 + k
            m = mixed_ref[o * 512 : (o + 1) * 512, :]
            g = dot(m, c_ref[:, o * 128 : (o + 1) * 128], 1, 0).reshape(32, 2, 8, 128)
            kept.append(jnp.where(first, g[:, 0], g[:, 1]))
            sent.append(jnp.where(first, g[:, 1], g[:, 0]))
        rows = slice(pair * 16, pair * 16 + 16)
        store_ordered(keep_ref, rows, jnp.concatenate(kept, axis=1).astype(BF16))
        store_ordered(send_ref, rows, jnp.concatenate(sent, axis=1).astype(BF16))


def call(kernel, name, args, outs, scratch):
    return pl.pallas_call(
        kernel,
        name=name,
        out_shape=[jax.ShapeDtypeStruct(shape, dtype) for shape, dtype in outs],
        in_specs=[SMEM] + [VMEM] * (len(args) - 1),
        out_specs=[VMEM] * len(outs),
        scratch_shapes=[pltpu.VMEM(shape, F32 if dtype is F32 else BF16) for shape, dtype in scratch],
        compiler_params=PARAMS,
        cost_estimate=pl.CostEstimate(
            flops=2 * 256 * 128 * 512 * 6, bytes_accessed=6_000_000, transcendentals=0
        ),
    )(*args)


def exchange(value, axis):
    return lax.all_to_all(value, axis, 0, 0, tiled=True)


def swap_cores(value):
    return lax.ppermute(value, "core", [(0, 1), (1, 0)])


def rotate(value, step):
    return lax.ppermute(value, MP, [(n, (n + step) % 8) for n in range(8)])


def add(first, second):
    return (first.astype(F32) + second.astype(F32)).astype(BF16)


def on_device(tokens, w_in, w_out, cotangent):
    scale = 1.0 / jnp.sqrt(F32(ROWS * 64))
    at = jnp.stack([lax.axis_index(MP), lax.axis_index("core")]).astype(jnp.int32)
    shard = jnp.concatenate(
        [w_in.transpose(1, 0, 2).reshape(48, 128), w_out.transpose(1, 0, 2).reshape(48, 128)]
    )
    along_z = lax.all_gather(shard, ("z_hi", "z_lo"), axis=0, tiled=False)
    mine = lax.all_gather(along_z, "x_hi", axis=0, tiled=False).reshape(32, 96, 128)
    other = swap_cores(mine)

    piece = (24, 16, ROWS)
    half = ((32, 48, 128), BF16)
    block = (NB, 512, ROWS)
    back_send, wout = call(
        back_kernel, "d_mixed", (at, mine, other, cotangent),
        [((8,) + piece, BF16), ((NB, 512, 128), BF16)],
        [((3072, 128), F32), ((3072, 128), F32)],
    )
    back = exchange(back_send, MP)
    *act, slope, win = call(
        forward_kernel, "act", (at, mine, other, tokens),
        [(piece, BF16)] * 8 + [(block, F32), ((NB, 128, 512), BF16)],
        [((1536, 128), F32), ((1536, 128), F32), ((4, 128, 128), F32), ((24, 8, 16, ROWS), BF16)],
    )
    moved = [act[0]] + [rotate(act[s], s) for s in range(1, 8)]
    d_pre, keep_in, send_in = call(
        first_grad_kernel, "first_grad", (at, back, slope, tokens),
        [(block, BF16), half, half],
        [((4, 128, 128), F32), ((2, 1536, 128), F32)],
    )
    half_in = add(keep_in, swap_cores(send_in))
    got_in = exchange(half_in.reshape(8, 192, 128), ("x_hi", "z_lo"))
    mixed, keep_out, send_out = call(
        second_grad_kernel, "second_grad", (at, *moved, cotangent),
        [((3072, ROWS), BF16), half, half],
        [((3072, 128), F32), ((3072, 128), F32)],
    )
    half_out = add(keep_out, swap_cores(send_out))
    got_out = exchange(half_out.reshape(8, 192, 128), ("x_hi", "z_lo"))
    both = jnp.concatenate(
        [g.astype(F32).sum(axis=0).astype(BF16).reshape(4, 48, 128) for g in (got_in, got_out)],
        axis=1,
    )
    total = exchange(both, "z_hi").astype(F32).sum(axis=0) * scale
    grad_in = total[:48].reshape(NB, 2, 512).transpose(1, 0, 2)
    grad_out = total[48:].reshape(NB, 8, 128).transpose(1, 0, 2)

    out = jnp.einsum("oet,oen->ton", mixed.reshape(block), wout, preferred_element_type=F32)
    output = out.astype(BF16).reshape(ROWS, 768)
    grad_x = jnp.einsum("iet,ire->tir", d_pre, win, preferred_element_type=F32)
    grad_tokens = grad_x.astype(BF16).reshape(ROWS, 768)
    return (output, grad_tokens, grad_in, grad_out)


def solution(mesh):
    fine = Mesh(mesh.devices.reshape(SIZES), DP + MP)
    placed = (P(DP, MP), P(DP, MP, None), P(DP, MP, None), P(DP, MP))
    return jax.shard_map(
        on_device,
        mesh=fine,
        in_specs=placed,
        out_specs=(P(DP, MP), P(DP, MP), P(DP, MP, None), P(DP, MP, None)),
        check_vma=False,
    )
```

```python
import jax
import jax.numpy as jnp
from jax import lax
from jax.experimental import pallas as pl
from jax.experimental.pallas import tpu as pltpu
from jax.sharding import Mesh, PartitionSpec as P

NB = 6
ROWS = 256
DP = ("x_hi", "z_hi", "z_lo", "core")
MP = ("x_lo", "y")
SIZES = (2, 4, 4, 2, 2, 4)
F32 = jnp.float32
BF16 = jnp.bfloat16
PARAMS = pltpu.CompilerParams(vmem_limit_bytes=20 * 1024 * 1024)
SMEM = pl.BlockSpec(memory_space=pltpu.SMEM)
ANY = pl.BlockSpec(memory_space=pl.ANY)
VMEM = pl.BlockSpec(memory_space=pltpu.VMEM)


def dot(lhs, rhs, lhs_dim, rhs_dim):
    return lax.dot_general(
        lhs, rhs, (((lhs_dim,), (rhs_dim,)), ((), ())), preferred_element_type=F32
    )


def halves(value, step):
    return value[:, step * 128 : (step + 1) * 128]


def back_kernel(at_ref, mine_ref, other_ref, c_ref, send_ref, wout_ref, left, right):
    first = at_ref[1] == 0
    for pair in range(NB // 2):
        rows = slice(48 + pair * 16, 48 + pair * 16 + 16)
        mine = mine_ref[:, rows, :].astype(F32)
        other = other_ref[:, rows, :].astype(F32)
        zero = jnp.where(first, mine, other)
        one = jnp.where(first, other, mine)
        for k in range(2):
            o = pair * 2 + k
            cut = slice(k * 8, k * 8 + 8)
            wide = jnp.stack([zero[:, cut], one[:, cut]], axis=1).reshape(512, 128)
            w = wide.astype(BF16)
            wout_ref[o] = w
            d = dot(w, c_ref[:, o * 128 : (o + 1) * 128], 1, 1)
            left[o * 512 : (o + 1) * 512, :] = d[:, :128]
            right[o * 512 : (o + 1) * 512, :] = d[:, 128:]
    for p in range(8):
        for g in range(24):
            at = pl.ds(p * 24 + g, 16, stride=192)
            send_ref[p, g, :, :128] = left[at, :].astype(BF16)
            send_ref[p, g, :, 128:] = right[at, :].astype(BF16)


def spread_kernel(x_ref, out_ref, moved, sems):
    row = lax.broadcasted_iota(jnp.int32, (256, 256), 0)
    col = lax.broadcasted_iota(jnp.int32, (256, 256), 1)
    source = (col // 64 % 2) * 128 + (col % 32) * 4 + (col // 128) * 2 + col // 32 % 2
    pick = jnp.where(row == source, 1.0, 0.0).astype(BF16)
    for pair in range(NB // 2):
        cut = slice(pair * 256, pair * 256 + 256)
        moved[:, cut] = dot(x_ref[:, cut], pick, 1, 0).astype(BF16)
    copies = [pltpu.make_async_copy(moved, out_ref.at[q], sems.at[q]) for q in range(8)]
    for copy in copies:
        copy.start()
    for copy in copies:
        copy.wait()


def columns_kernel(mine_ref, after_ref, send_ref, mine_f):
    mine_f[...] = mine_ref[:, :48, :].astype(F32).reshape(32 * 48, 128)
    for pair in range(NB // 2):
        for c in range(4):
            rows = [
                mine_f[pl.ds((pair * 2 + i) * 8 + k * 4 + c, 32, stride=48), :]
                for i in range(2)
                for k in range(2)
            ]
            turned = jnp.concatenate(rows, axis=0).T.astype(BF16)
            for q in range(8):
                send_ref[q, pair, c * 16 : (c + 1) * 16, :] = turned[q * 16 : (q + 1) * 16]


ROOT = 0.7978845608028654


def slope_kernel(at_ref, mine_ref, other_ref, x_ref, slope_ref, win_ref, mine_f, other_f, w_f):
    first = at_ref[1] == 0
    mine_f[...] = mine_ref[:, :48, :].astype(F32).reshape(32 * 48, 128)
    other_f[...] = other_ref[:, :48, :].astype(F32).reshape(32 * 48, 128)
    for i in range(NB):
        for k in range(2):
            for c in range(4):
                at = pl.ds(i * 8 + k * 4 + c, 32, stride=48)
                mine, other = mine_f[at, :], other_f[at, :]
                w_f[c, pl.ds(k, 32, stride=4), :] = jnp.where(first, mine, other)
                w_f[c, pl.ds(2 + k, 32, stride=4), :] = jnp.where(first, other, mine)
        for c in range(4):
            w = w_f[c].astype(BF16)
            win_ref[i, :, c * 128 : (c + 1) * 128] = w
            v = dot(w, x_ref[:, i * 128 : (i + 1) * 128], 0, 1)
            square = v * v
            th = jnp.tanh(ROOT * (v + 0.044715 * (v * square)))
            slope_ref[i, c * 128 : (c + 1) * 128, :] = 0.5 * (1.0 + th) + (0.5 * ROOT) * v * (
                1.0 - th * th
            ) * (1.0 + 0.134145 * square)


def store_ordered(ref, rows, value):
    for n in range(32):
        ref[n // 16 * 16 + n % 4 * 4 + n // 4 % 4, rows, :] = value[n]


def first_grad_kernel(at_ref, back_ref, slope_ref, x_ref, after_ref, dpre_ref, keep_ref, send_ref, p_f, o_f):
    first = at_ref[1] == 0
    for i in range(NB):
        parts = [back_ref[:, i * 4 + a].reshape(128, ROWS) for a in range(4)]
        x = x_ref[:, i * 128 : (i + 1) * 128]
        for c in range(4):
            d = (parts[c].astype(F32) * slope_ref[i, c * 128 : (c + 1) * 128, :]).astype(BF16)
            dpre_ref[i, c * 128 : (c + 1) * 128, :] = d
            p_f[c] = dot(x, d, 0, 1)
            for core in range(2):
                for k in range(2):
                    o_f[core, pl.ds(i * 8 + k * 4 + c, 32, stride=48), :] = p_f[
                        c, pl.ds(core * 2 + k, 32, stride=4), :
                    ]
    zero = o_f[0].reshape(32, 48, 128)
    one = o_f[1].reshape(32, 48, 128)
    store_ordered(keep_ref, slice(0, 48), jnp.where(first, zero, one).astype(BF16))
    store_ordered(send_ref, slice(0, 48), jnp.where(first, one, zero).astype(BF16))


def second_grad_kernel(
    at_ref, x_ref, mine_ref, other_ref, c_ref, mixed_ref, keep_ref, send_ref, left, right
):
    first = at_ref[1] == 0
    lane = lax.broadcasted_iota(jnp.int32, (64, 128), 1) < 64
    zero = jnp.zeros((64, 128), F32)
    for p in range(8):
        for pair in range(NB // 2):
            mine = mine_ref[p, pair].astype(F32)
            other = other_ref[p, pair].astype(F32)
            v = None
            for core in range(2):
                w = jnp.where(first, mine, other) if core == 0 else jnp.where(first, other, mine)
                w = jnp.concatenate([jnp.where(lane, w, zero), jnp.where(lane, zero, w)])
                cut = slice(pair * 256 + core * 128, pair * 256 + core * 128 + 128)
                part = dot(w.astype(BF16), x_ref[p, :, cut], 1, 1)
                v = part if v is None else v + part
            th = jnp.tanh(ROOT * (v + 0.044715 * (v * (v * v))))
            act = (0.5 * v) * (1.0 + th)
            start = (p * 3 + pair) * 128
            left[start : start + 128, :] = act[:, :128]
            right[start : start + 128, :] = act[:, 128:]
    for j in range(16):
        at = pl.ds(j, 192, stride=16)
        mixed_ref[j * 192 : (j + 1) * 192, :128] = left[at, :].astype(BF16)
        mixed_ref[j * 192 : (j + 1) * 192, 128:] = right[at, :].astype(BF16)
    for pair in range(NB // 2):
        kept, sent = [], []
        for k in range(2):
            o = pair * 2 + k
            m = mixed_ref[o * 512 : (o + 1) * 512, :]
            g = dot(m, c_ref[:, o * 128 : (o + 1) * 128], 1, 0).reshape(32, 2, 8, 128)
            kept.append(jnp.where(first, g[:, 0], g[:, 1]))
            sent.append(jnp.where(first, g[:, 1], g[:, 0]))
        rows = slice(pair * 16, pair * 16 + 16)
        store_ordered(keep_ref, rows, jnp.concatenate(kept, axis=1).astype(BF16))
        store_ordered(send_ref, rows, jnp.concatenate(sent, axis=1).astype(BF16))


def call(kernel, name, args, outs, scratch=(), unread=()):
    return pl.pallas_call(
        kernel,
        name=name,
        out_shape=[jax.ShapeDtypeStruct(shape, dtype) for shape, dtype in outs],
        in_specs=[
            ANY if n in unread else SMEM if arg.ndim == 1 else VMEM for n, arg in enumerate(args)
        ],
        out_specs=[VMEM] * len(outs),
        scratch_shapes=[pltpu.VMEM(shape, F32 if dtype is F32 else BF16) for shape, dtype in scratch],
        compiler_params=PARAMS,
        cost_estimate=pl.CostEstimate(
            flops=2 * 256 * 128 * 512 * 6, bytes_accessed=6_000_000, transcendentals=0
        ),
    )(*args)


def join_kernel(keep_in, got_in, keep_out, got_out, both_ref):
    both_ref[:, :48, :] = (keep_in[...].astype(F32) + got_in[...].astype(F32)).astype(BF16)
    both_ref[:, 48:, :] = (keep_out[...].astype(F32) + got_out[...].astype(F32)).astype(BF16)


def exchange(value, axis):
    return lax.all_to_all(value, axis, 0, 0, tiled=True)


def swap_cores(value):
    return lax.ppermute(value, "core", [(0, 1), (1, 0)])


def on_device(tokens, w_in, w_out, cotangent):
    scale = 1.0 / jnp.sqrt(F32(ROWS * 64))
    at = jnp.stack([lax.axis_index(MP), lax.axis_index("core")]).astype(jnp.int32)
    shard = jnp.concatenate(
        [w_in.transpose(1, 0, 2).reshape(48, 128), w_out.transpose(1, 0, 2).reshape(48, 128)]
    )
    copies = pl.pallas_call(
        spread_kernel,
        name="spread",
        out_shape=jax.ShapeDtypeStruct((8, ROWS, 768), BF16),
        in_specs=[VMEM],
        out_specs=pl.BlockSpec(memory_space=pltpu.HBM),
        scratch_shapes=[pltpu.VMEM((ROWS, 768), BF16), pltpu.SemaphoreType.DMA((8,))],
        compiler_params=PARAMS,
    )(tokens)
    gathered = exchange(copies, MP)
    along_z = lax.all_gather(shard, ("z_hi", "z_lo"), axis=0, tiled=False)
    mine = lax.all_gather(along_z, "x_hi", axis=0, tiled=False).reshape(32, 96, 128)
    other = swap_cores(mine)

    half = ((32, 48, 128), BF16)
    block = (NB, 512, ROWS)
    (column_send,) = call(
        columns_kernel, "columns", (mine, gathered), [((8, 3, 64, 128), BF16)], [((1536, 128), F32)], (1,)
    )
    columns = exchange(column_send, MP)
    other_columns = swap_cores(columns)
    back_send, wout = call(
        back_kernel, "d_mixed", (at, mine, other, cotangent),
        [((8, 24, 16, ROWS), BF16), ((NB, 512, 128), BF16)],
        [((3072, 128), F32), ((3072, 128), F32)],
    )
    back = exchange(back_send, MP)
    mixed, keep_out, send_out = call(
        second_grad_kernel, "second_grad", (at, gathered, columns, other_columns, cotangent),
        [((3072, ROWS), BF16), half, half],
        [((3072, 128), F32), ((3072, 128), F32)],
    )
    got_out = swap_cores(send_out)
    slope, win = call(
        slope_kernel, "slope", (at, mine, other, tokens),
        [(block, F32), ((NB, 128, 512), BF16)],
        [((1536, 128), F32), ((1536, 128), F32), ((4, 128, 128), F32)],
    )
    d_pre, keep_in, send_in = call(
        first_grad_kernel, "first_grad", (at, back, slope, tokens, got_out),
        [(block, BF16), half, half],
        [((4, 128, 128), F32), ((2, 1536, 128), F32)],
        (4,),
    )
    got_in = swap_cores(send_in)
    (both,) = call(
        join_kernel, "join", (keep_in, got_in, keep_out, got_out), [((32, 96, 128), BF16)]
    )
    got = exchange(both.reshape(8, 384, 128), ("x_hi", "z_lo"))
    both = got.astype(F32).sum(axis=0).astype(BF16).reshape(4, 96, 128)
    total = exchange(both, "z_hi").astype(F32).sum(axis=0) * scale
    grad_in = total[:48].reshape(NB, 2, 512).transpose(1, 0, 2)
    grad_out = total[48:].reshape(NB, 8, 128).transpose(1, 0, 2)

    out = jnp.einsum("oet,oen->ton", mixed.reshape(block), wout, preferred_element_type=F32)
    output = out.astype(BF16).reshape(ROWS, 768)
    grad_x = jnp.einsum("iet,ire->tir", d_pre, win, preferred_element_type=F32)
    grad_tokens = grad_x.astype(BF16).reshape(ROWS, 768)
    return (output, grad_tokens, grad_in, grad_out)


def solution(mesh):
    fine = Mesh(mesh.devices.reshape(SIZES), DP + MP)
    placed = (P(DP, MP), P(DP, MP, None), P(DP, MP, None), P(DP, MP))
    return jax.shard_map(
        on_device,
        mesh=fine,
        in_specs=placed,
        out_specs=(P(DP, MP), P(DP, MP), P(DP, MP, None), P(DP, MP, None)),
        check_vma=False,
    )
```

```python
import jax
import jax.numpy as jnp
from jax import lax
from jax.experimental import pallas as pl
from jax.experimental.pallas import tpu as pltpu
from jax.sharding import Mesh, PartitionSpec as P

NB = 6
ROWS = 256
DP = ("x_hi", "z_hi", "z_lo", "core")
MP = ("x_lo", "y")
SIZES = (2, 4, 4, 2, 2, 4)
F32 = jnp.float32
BF16 = jnp.bfloat16
PARAMS = pltpu.CompilerParams(vmem_limit_bytes=20 * 1024 * 1024)
SMEM = pl.BlockSpec(memory_space=pltpu.SMEM)
ANY = pl.BlockSpec(memory_space=pl.ANY)
VMEM = pl.BlockSpec(memory_space=pltpu.VMEM)


def dot(lhs, rhs, lhs_dim, rhs_dim):
    return lax.dot_general(
        lhs, rhs, (((lhs_dim,), (rhs_dim,)), ((), ())), preferred_element_type=F32
    )


def halves(value, step):
    return value[:, step * 128 : (step + 1) * 128]


def back_kernel(at_ref, mine_ref, other_ref, c_ref, send_ref, wout_ref, left, right):
    first = at_ref[1] == 0
    for pair in range(NB // 2):
        rows = slice(48 + pair * 16, 48 + pair * 16 + 16)
        mine = mine_ref[:, rows, :].astype(F32)
        other = other_ref[:, rows, :].astype(F32)
        zero = jnp.where(first, mine, other)
        one = jnp.where(first, other, mine)
        for k in range(2):
            o = pair * 2 + k
            cut = slice(k * 8, k * 8 + 8)
            wide = jnp.stack([zero[:, cut], one[:, cut]], axis=1).reshape(512, 128)
            w = wide.astype(BF16)
            wout_ref[o] = w
            d = dot(w, c_ref[:, o * 128 : (o + 1) * 128], 1, 1)
            left[o * 512 : (o + 1) * 512, :] = d[:, :128]
            right[o * 512 : (o + 1) * 512, :] = d[:, 128:]
    for p in range(8):
        for g in range(24):
            at = pl.ds(p * 24 + g, 16, stride=192)
            send_ref[p, g, :, :128] = left[at, :].astype(BF16)
            send_ref[p, g, :, 128:] = right[at, :].astype(BF16)


def columns_kernel(mine_ref, after_ref, send_ref, relay_ref, mine_f):
    for x in range(2):
        rows = mine_ref[:, x]
        relay_ref[x * 16 : (x + 1) * 16] = rows
        mine_f[x * 768 : (x + 1) * 768, :] = rows[:, :48].astype(F32).reshape(768, 128)
    for pair in range(NB // 2):
        for c in range(4):
            rows = [
                mine_f[pl.ds((pair * 2 + i) * 8 + k * 4 + c, 32, stride=48), :]
                for i in range(2)
                for k in range(2)
            ]
            turned = jnp.concatenate(rows, axis=0).T.astype(BF16)
            for q in range(8):
                send_ref[q, pair, c * 16 : (c + 1) * 16, :] = turned[q * 16 : (q + 1) * 16]


ROOT = 0.7978845608028654


def slope_kernel(at_ref, mine_ref, other_ref, x_ref, slope_ref, win_ref, mine_f, other_f, w_f):
    first = at_ref[1] == 0
    mine_f[...] = mine_ref[:, :48, :].astype(F32).reshape(32 * 48, 128)
    other_f[...] = other_ref[:, :48, :].astype(F32).reshape(32 * 48, 128)
    for i in range(NB):
        for k in range(2):
            for c in range(4):
                at = pl.ds(i * 8 + k * 4 + c, 32, stride=48)
                mine, other = mine_f[at, :], other_f[at, :]
                w_f[c, pl.ds(k, 32, stride=4), :] = jnp.where(first, mine, other)
                w_f[c, pl.ds(2 + k, 32, stride=4), :] = jnp.where(first, other, mine)
        for c in range(4):
            w = w_f[c].astype(BF16)
            win_ref[i, :, c * 128 : (c + 1) * 128] = w
            v = dot(w, x_ref[:, i * 128 : (i + 1) * 128], 0, 1)
            square = v * v
            th = jnp.tanh(ROOT * (v + 0.044715 * (v * square)))
            slope_ref[i, c * 128 : (c + 1) * 128, :] = 0.5 * (1.0 + th) + (0.5 * ROOT) * v * (
                1.0 - th * th
            ) * (1.0 + 0.134145 * square)


def store_ordered(ref, rows, value):
    for n in range(32):
        ref[n // 16 * 16 + n % 4 * 4 + n // 4 % 4, rows, :] = value[n]


def first_grad_kernel(at_ref, back_ref, slope_ref, x_ref, after_ref, dpre_ref, keep_ref, send_ref, p_f, o_f):
    first = at_ref[1] == 0
    for i in range(NB):
        parts = [back_ref[:, i * 4 + a].reshape(128, ROWS) for a in range(4)]
        x = x_ref[:, i * 128 : (i + 1) * 128]
        for c in range(4):
            d = (parts[c].astype(F32) * slope_ref[i, c * 128 : (c + 1) * 128, :]).astype(BF16)
            dpre_ref[i, c * 128 : (c + 1) * 128, :] = d
            p_f[c] = dot(x, d, 0, 1)
            for core in range(2):
                for k in range(2):
                    o_f[core, pl.ds(i * 8 + k * 4 + c, 32, stride=48), :] = p_f[
                        c, pl.ds(core * 2 + k, 32, stride=4), :
                    ]
    zero = o_f[0].reshape(32, 48, 128)
    one = o_f[1].reshape(32, 48, 128)
    store_ordered(keep_ref, slice(0, 48), jnp.where(first, zero, one).astype(BF16))
    store_ordered(send_ref, slice(0, 48), jnp.where(first, one, zero).astype(BF16))


def second_grad_kernel(
    at_ref, x_ref, mine_ref, other_ref, c_ref, mixed_ref, keep_ref, send_ref, left, right
):
    first = at_ref[1] == 0
    row = lax.broadcasted_iota(jnp.int32, (256, 256), 0)
    col = lax.broadcasted_iota(jnp.int32, (256, 256), 1)
    target = (row // 64 % 2) * 128 + (row % 32) * 4 + (row // 128) * 2 + row // 32 % 2
    place = jnp.where(col == target, 1.0, 0.0).astype(BF16)
    for p in range(8):
        mine = mine_ref[p].reshape(192, 128).astype(F32)
        other = other_ref[p].reshape(192, 128).astype(F32)
        w = jnp.concatenate(
            [jnp.where(first, mine, other), jnp.where(first, other, mine)], axis=1
        ).astype(BF16)
        w = dot(w, place, 1, 0).astype(BF16)
        for i in range(NB):
            rows = slice(i // 2 * 64, i // 2 * 64 + 64)
            v = dot(
                w[rows, i % 2 * 128 : i % 2 * 128 + 128], x_ref[p, :, i * 128 : (i + 1) * 128], 1, 1
            )
            th = jnp.tanh(ROOT * (v + 0.044715 * (v * (v * v))))
            act = (0.5 * v) * (1.0 + th)
            start = (p * NB + i) * 64
            left[start : start + 64, :] = act[:, :128]
            right[start : start + 64, :] = act[:, 128:]
    for j in range(16):
        at = pl.ds(j, 192, stride=16)
        mixed_ref[j * 192 : (j + 1) * 192, :128] = left[at, :].astype(BF16)
        mixed_ref[j * 192 : (j + 1) * 192, 128:] = right[at, :].astype(BF16)
    for pair in range(NB // 2):
        kept, sent = [], []
        for k in range(2):
            o = pair * 2 + k
            m = mixed_ref[o * 512 : (o + 1) * 512, :]
            g = dot(m, c_ref[:, o * 128 : (o + 1) * 128], 1, 0).reshape(32, 2, 8, 128)
            kept.append(jnp.where(first, g[:, 0], g[:, 1]))
            sent.append(jnp.where(first, g[:, 1], g[:, 0]))
        rows = slice(pair * 16, pair * 16 + 16)
        store_ordered(keep_ref, rows, jnp.concatenate(kept, axis=1).astype(BF16))
        store_ordered(send_ref, rows, jnp.concatenate(sent, axis=1).astype(BF16))


def call(kernel, name, args, outs, scratch=(), unread=()):
    return pl.pallas_call(
        kernel,
        name=name,
        out_shape=[jax.ShapeDtypeStruct(shape, dtype) for shape, dtype in outs],
        in_specs=[
            ANY if n in unread else SMEM if arg.ndim == 1 else VMEM for n, arg in enumerate(args)
        ],
        out_specs=[VMEM] * len(outs),
        scratch_shapes=[pltpu.VMEM(shape, F32 if dtype is F32 else BF16) for shape, dtype in scratch],
        compiler_params=PARAMS,
        cost_estimate=pl.CostEstimate(
            flops=2 * 256 * 128 * 512 * 6, bytes_accessed=6_000_000, transcendentals=0
        ),
    )(*args)


def join_kernel(keep_in, got_in, keep_out, got_out, both_ref):
    both_ref[:, :48, :] = (keep_in[...].astype(F32) + got_in[...].astype(F32)).astype(BF16)
    both_ref[:, 48:, :] = (keep_out[...].astype(F32) + got_out[...].astype(F32)).astype(BF16)


def exchange(value, axis):
    return lax.all_to_all(value, axis, 0, 0, tiled=True)


def swap_cores(value):
    return lax.ppermute(value, "core", [(0, 1), (1, 0)])


def on_device(tokens, w_in, w_out, cotangent):
    scale = 1.0 / jnp.sqrt(F32(ROWS * 64))
    at = jnp.stack([lax.axis_index(MP), lax.axis_index("core")]).astype(jnp.int32)
    shard = jnp.concatenate(
        [w_in.transpose(1, 0, 2).reshape(48, 128), w_out.transpose(1, 0, 2).reshape(48, 128)]
    )
    sent, _ = lax.optimization_barrier((tokens, shard))
    gathered = exchange(jnp.broadcast_to(sent[None], (8, ROWS, 768)), MP)
    pair = lax.all_gather(shard, "x_hi", axis=0, tiled=False)
    along_z = lax.all_gather(pair, ("z_hi", "z_lo"), axis=0, tiled=False)

    half = ((32, 48, 128), BF16)
    block = (NB, 512, ROWS)
    column_send, mine = call(
        columns_kernel, "columns", (along_z, gathered),
        [((8, 3, 64, 128), BF16), ((32, 96, 128), BF16)], [((1536, 128), F32)], (1,)
    )
    other = swap_cores(mine)
    columns = exchange(column_send, MP)
    other_columns = swap_cores(columns)
    back_send, wout = call(
        back_kernel, "d_mixed", (at, mine, other, cotangent),
        [((8, 24, 16, ROWS), BF16), ((NB, 512, 128), BF16)],
        [((3072, 128), F32), ((3072, 128), F32)],
    )
    back = exchange(back_send, MP)
    mixed, keep_out, send_out = call(
        second_grad_kernel, "second_grad", (at, gathered, columns, other_columns, cotangent),
        [((3072, ROWS), BF16), half, half],
        [((3072, 128), F32), ((3072, 128), F32)],
    )
    got_out = swap_cores(send_out)
    slope, win = call(
        slope_kernel, "slope", (at, mine, other, tokens),
        [(block, F32), ((NB, 128, 512), BF16)],
        [((1536, 128), F32), ((1536, 128), F32), ((4, 128, 128), F32)],
    )
    d_pre, keep_in, send_in = call(
        first_grad_kernel, "first_grad", (at, back, slope, tokens, got_out),
        [(block, BF16), half, half],
        [((4, 128, 128), F32), ((2, 1536, 128), F32)],
        (4,),
    )
    got_in = swap_cores(send_in)
    (both,) = call(
        join_kernel, "join", (keep_in, got_in, keep_out, got_out), [((32, 96, 128), BF16)]
    )
    got = exchange(both.reshape(8, 384, 128), ("x_hi", "z_lo"))
    both = got.astype(F32).sum(axis=0).astype(BF16).reshape(4, 96, 128)
    total = exchange(both, "z_hi").astype(F32).sum(axis=0) * scale
    grad_in = total[:48].reshape(NB, 2, 512).transpose(1, 0, 2)
    grad_out = total[48:].reshape(NB, 8, 128).transpose(1, 0, 2)

    out = jnp.einsum("oet,oen->ton", mixed.reshape(block), wout, preferred_element_type=F32)
    output = out.astype(BF16).reshape(ROWS, 768)
    grad_x = jnp.einsum("iet,ire->tir", d_pre, win, preferred_element_type=F32)
    grad_tokens = grad_x.astype(BF16).reshape(ROWS, 768)
    return (output, grad_tokens, grad_in, grad_out)


def solution(mesh):
    fine = Mesh(mesh.devices.reshape(SIZES), DP + MP)
    placed = (P(DP, MP), P(DP, MP, None), P(DP, MP, None), P(DP, MP))
    return jax.shard_map(
        on_device,
        mesh=fine,
        in_specs=placed,
        out_specs=(P(DP, MP), P(DP, MP), P(DP, MP, None), P(DP, MP, None)),
        check_vma=False,
    )
```

```python
import jax
import jax.numpy as jnp
from jax import lax
from jax.experimental import pallas as pl
from jax.experimental.pallas import tpu as pltpu
from jax.sharding import Mesh, PartitionSpec as P

NB = 6
ROWS = 256
DP = ("x_hi", "z", "core")
MP = ("x_lo", "y")
SIZES = (2, 16, 2, 2, 4)
F32 = jnp.float32
BF16 = jnp.bfloat16
PARAMS = pltpu.CompilerParams(vmem_limit_bytes=20 * 1024 * 1024)
SMEM = pl.BlockSpec(memory_space=pltpu.SMEM)
ANY = pl.BlockSpec(memory_space=pl.ANY)
VMEM = pl.BlockSpec(memory_space=pltpu.VMEM)


def dot(lhs, rhs, lhs_dim, rhs_dim):
    return lax.dot_general(
        lhs, rhs, (((lhs_dim,), (rhs_dim,)), ((), ())), preferred_element_type=F32
    )


def halves(value, step):
    return value[:, step * 128 : (step + 1) * 128]


def shard_rows(ref, rows):
    return jnp.concatenate([ref[:, 0, rows], ref[:, 1, rows]], axis=0).astype(F32)


def second_factor(first, mine_ref, other_ref, pair):
    rows = slice(48 + pair * 16, 48 + pair * 16 + 16)
    mine, other = shard_rows(mine_ref, rows), shard_rows(other_ref, rows)
    zero = jnp.where(first, mine, other)
    one = jnp.where(first, other, mine)
    return [
        jnp.stack([zero[:, cut], one[:, cut]], axis=1).reshape(512, 128).astype(BF16)
        for cut in (slice(0, 8), slice(8, 16))
    ]


def back_kernel(at_ref, mine_ref, other_ref, c_ref, send_ref, left, right):
    first = at_ref[1] == 0
    for pair in range(NB // 2):
        for k, w in enumerate(second_factor(first, mine_ref, other_ref, pair)):
            o = pair * 2 + k
            d = dot(w, c_ref[:, o * 128 : (o + 1) * 128], 1, 1)
            left[o * 512 : (o + 1) * 512, :] = d[:, :128]
            right[o * 512 : (o + 1) * 512, :] = d[:, 128:]
    for p in range(8):
        for g in range(24):
            at = pl.ds(p * 24 + g, 16, stride=192)
            send_ref[p, g, :, :128] = left[at, :].astype(BF16)
            send_ref[p, g, :, 128:] = right[at, :].astype(BF16)


def columns_kernel(mine_ref, send_ref, mine_f):
    mine_f[...] = shard_rows(mine_ref, slice(0, 48)).reshape(32 * 48, 128)
    for pair in range(NB // 2):
        for c in range(4):
            rows = [
                mine_f[pl.ds((pair * 2 + i) * 8 + k * 4 + c, 32, stride=48), :]
                for i in range(2)
                for k in range(2)
            ]
            turned = jnp.concatenate(rows, axis=0).T.astype(BF16)
            for q in range(8):
                send_ref[q, pair, c * 16 : (c + 1) * 16, :] = turned[q * 16 : (q + 1) * 16]


ROOT = 0.7978845608028654


def first_grad_kernel(
    at_ref, mine_ref, other_ref, x_ref, back_ref, after_ref, gx_ref, keep_ref, send_ref,
    mine_f, other_f, w_f, p_f, o_f,
):
    first = at_ref[1] == 0
    mine_f[...] = shard_rows(mine_ref, slice(0, 48)).reshape(32 * 48, 128)
    other_f[...] = shard_rows(other_ref, slice(0, 48)).reshape(32 * 48, 128)
    for i in range(NB):
        for k in range(2):
            for c in range(4):
                at = pl.ds(i * 8 + k * 4 + c, 32, stride=48)
                mine, other = mine_f[at, :], other_f[at, :]
                w_f[c, pl.ds(k, 32, stride=4), :] = jnp.where(first, mine, other)
                w_f[c, pl.ds(2 + k, 32, stride=4), :] = jnp.where(first, other, mine)
        x = x_ref[:, i * 128 : (i + 1) * 128].T
        gx = None
        for c in range(4):
            w = w_f[c].astype(BF16)
            v = dot(w, x, 0, 0)
            square = v * v
            th = jnp.tanh(ROOT * (v + 0.044715 * (v * square)))
            slope = 0.5 * (1.0 + th) + (0.5 * ROOT) * v * (1.0 - th * th) * (1.0 + 0.134145 * square)
            d = (back_ref[:, i * 4 + c].reshape(128, ROWS).astype(F32) * slope).astype(BF16)
            part = dot(w, d, 1, 0)
            gx = part if gx is None else gx + part
            p_f[c] = dot(x, d, 1, 1)
            for core in range(2):
                for k in range(2):
                    o_f[core, pl.ds(i * 8 + k * 4 + c, 32, stride=48), :] = p_f[
                        c, pl.ds(core * 2 + k, 32, stride=4), :
                    ]
        gx_ref[:, i * 128 : (i + 1) * 128] = gx.T.astype(BF16)
    zero = o_f[0].reshape(32, 48, 128)
    one = o_f[1].reshape(32, 48, 128)
    keep_ref[...] = jnp.where(first, zero, one).astype(BF16)
    send_ref[...] = jnp.where(first, one, zero).astype(BF16)


def second_grad_kernel(
    at_ref, x_ref, mine_ref, other_ref, c_ref, wmine_ref, wother_ref, out_ref, keep_ref,
    send_ref, mixed_ref, left, right,
):
    first = at_ref[1] == 0
    row = lax.broadcasted_iota(jnp.int32, (256, 256), 0)
    col = lax.broadcasted_iota(jnp.int32, (256, 256), 1)
    target = (row // 64 % 2) * 128 + (row % 32) * 4 + (row // 128) * 2 + row // 32 % 2
    place = jnp.where(col == target, 1.0, 0.0).astype(BF16)
    for p in range(8):
        mine = mine_ref[p].reshape(192, 128).astype(F32)
        other = other_ref[p].reshape(192, 128).astype(F32)
        w = jnp.concatenate(
            [jnp.where(first, mine, other), jnp.where(first, other, mine)], axis=1
        ).astype(BF16)
        w = dot(w, place, 1, 0).astype(BF16)
        for i in range(NB):
            rows = slice(i // 2 * 64, i // 2 * 64 + 64)
            v = dot(
                w[rows, i % 2 * 128 : i % 2 * 128 + 128], x_ref[p, :, i * 128 : (i + 1) * 128], 1, 1
            )
            th = jnp.tanh(ROOT * (v + 0.044715 * (v * (v * v))))
            act = (0.5 * v) * (1.0 + th)
            start = (p * NB + i) * 64
            left[start : start + 64, :] = act[:, :128]
            right[start : start + 64, :] = act[:, 128:]
    for j in range(16):
        at = pl.ds(j, 192, stride=16)
        mixed_ref[j * 192 : (j + 1) * 192, :128] = left[at, :].astype(BF16)
        mixed_ref[j * 192 : (j + 1) * 192, 128:] = right[at, :].astype(BF16)
    for pair in range(NB // 2):
        kept, sent = [], []
        wout = second_factor(first, wmine_ref, wother_ref, pair)
        for k in range(2):
            o = pair * 2 + k
            m = mixed_ref[o * 512 : (o + 1) * 512, :]
            out_ref[:, o * 128 : (o + 1) * 128] = dot(m, wout[k], 0, 0).astype(BF16)
            g = dot(m, c_ref[:, o * 128 : (o + 1) * 128], 1, 0).reshape(32, 2, 8, 128)
            kept.append(jnp.where(first, g[:, 0], g[:, 1]))
            sent.append(jnp.where(first, g[:, 1], g[:, 0]))
        rows = slice(pair * 16, pair * 16 + 16)
        keep_ref[:, rows, :] = jnp.concatenate(kept, axis=1).astype(BF16)
        send_ref[:, rows, :] = jnp.concatenate(sent, axis=1).astype(BF16)


def call(kernel, name, args, outs, scratch=(), unread=()):
    return pl.pallas_call(
        kernel,
        name=name,
        out_shape=[jax.ShapeDtypeStruct(shape, dtype) for shape, dtype in outs],
        in_specs=[
            ANY if n in unread else SMEM if arg.ndim == 1 else VMEM for n, arg in enumerate(args)
        ],
        out_specs=[VMEM] * len(outs),
        scratch_shapes=[pltpu.VMEM(shape, F32 if dtype is F32 else BF16) for shape, dtype in scratch],
        compiler_params=PARAMS,
        cost_estimate=pl.CostEstimate(
            flops=2 * 256 * 128 * 512 * 6, bytes_accessed=6_000_000, transcendentals=0
        ),
    )(*args)


def join_kernel(at_ref, keep_in, got_in, keep_out, got_out, both_ref):
    for n in range(32):
        place = lax.rem(n % 4 + 2 * at_ref[1], 4)
        to = n // 16 * 16 + place * 4 + n // 4 % 4
        both_ref[to, :48, :] = (keep_in[n].astype(F32) + got_in[n].astype(F32)).astype(BF16)
        both_ref[to, 48:, :] = (keep_out[n].astype(F32) + got_out[n].astype(F32)).astype(BF16)


def part_kernel(got_ref, part_ref):
    total = got_ref[0].astype(F32)
    for n in range(1, 8):
        total = total + got_ref[n].astype(F32)
    part_ref[...] = total.astype(BF16)


def total_kernel(got_ref, in_ref, out_ref):
    total = got_ref[0].astype(F32)
    for n in range(1, 4):
        total = total + got_ref[n].astype(F32)
    total = total * (1.0 / 128.0)
    out_ref[...] = total[48:].reshape(NB, 8, 128)
    for i in range(NB):
        for k in range(2):
            for c in range(4):
                row = i * 8 + k * 4 + c
                in_ref[i, k : k + 1, c * 128 : (c + 1) * 128] = total[row : row + 1]


NEAR = [
    [x * 32 + (run * 4 + 2 * core + n) % 16 * 2 + core for x in range(2) for n in range(4)]
    for core in range(2)
    for run in range(4)
]
FAR = [
    [x * 32 + (run * 4 + n) * 2 + core for run in range(4)]
    for x in range(2)
    for n in range(4)
    for core in range(2)
]


def exchange(value, axis, groups=None):
    return lax.all_to_all(value, axis, 0, 0, axis_index_groups=groups, tiled=True)


def swap_cores(value):
    return lax.ppermute(value, "core", [(0, 1), (1, 0)])


def on_device(tokens, w_in, w_out, cotangent):
    at = jnp.stack([lax.axis_index(MP), lax.axis_index("core")]).astype(jnp.int32)
    shard = jnp.concatenate(
        [w_in.transpose(1, 0, 2).reshape(48, 128), w_out.transpose(1, 0, 2).reshape(48, 128)]
    )
    pair = lax.all_gather(shard, "x_hi", axis=0, tiled=False)
    sent, pair = lax.optimization_barrier((tokens, pair))
    gathered = exchange(jnp.broadcast_to(sent[None], (8, ROWS, 768)), MP)
    mine = lax.all_gather(pair, "z", axis=0, tiled=False)
    other = swap_cores(mine)

    half = ((32, 48, 128), BF16)
    (column_send,) = call(
        columns_kernel, "columns", (mine,), [((8, 3, 64, 128), BF16)], [((1536, 128), F32)]
    )
    column_send, gathered = lax.optimization_barrier((column_send, gathered))
    columns = exchange(column_send, MP)
    other_columns = swap_cores(columns)
    (back_send,) = call(
        back_kernel, "d_mixed", (at, mine, other, cotangent),
        [((8, 24, 16, ROWS), BF16)],
        [((3072, 128), F32), ((3072, 128), F32)],
    )
    back = exchange(back_send, MP)
    output, keep_out, send_out = call(
        second_grad_kernel, "second_grad",
        (at, gathered, columns, other_columns, cotangent, mine, other),
        [((ROWS, 768), BF16), half, half],
        [((3072, ROWS), BF16), ((3072, 128), F32), ((3072, 128), F32)],
    )
    got_out = swap_cores(send_out)
    grad_tokens, keep_in, send_in = call(
        first_grad_kernel, "first_grad", (at, mine, other, tokens, back, got_out),
        [((ROWS, 768), BF16), half, half],
        [((1536, 128), F32)] * 2 + [((4, 128, 128), F32)] * 2 + [((2, 1536, 128), F32)],
        (5,),
    )
    got_in = swap_cores(send_in)
    (both,) = call(
        join_kernel, "join", (at, keep_in, got_in, keep_out, got_out), [((32, 96, 128), BF16)]
    )
    near = exchange(both.reshape(8, 4, 96, 128), DP, NEAR)
    (part,) = call(part_kernel, "part", (near,), [((4, 96, 128), BF16)])
    grad_in, grad_out = call(
        total_kernel, "total", (exchange(part, DP, FAR),),
        [((NB, 2, 512), F32), ((NB, 8, 128), F32)],
    )
    grad_in, grad_out = grad_in.transpose(1, 0, 2), grad_out.transpose(1, 0, 2)
    return (output, grad_tokens, grad_in, grad_out)


def solution(mesh):
    fine = Mesh(mesh.devices.reshape(SIZES), DP + MP)
    placed = (P(DP, MP), P(DP, MP, None), P(DP, MP, None), P(DP, MP))
    return jax.shard_map(
        on_device,
        mesh=fine,
        in_specs=placed,
        out_specs=(P(DP, MP), P(DP, MP), P(DP, MP, None), P(DP, MP, None)),
        check_vma=False,
    )
```

```python
import jax
import jax.numpy as jnp
from jax import lax
from jax.experimental import pallas as pl
from jax.experimental.pallas import tpu as pltpu
from jax.sharding import Mesh, PartitionSpec as P

NB = 6
ROWS = 256
DP = ("x_hi", "z", "core")
MP = ("x_lo", "y")
SIZES = (2, 16, 2, 2, 4)
F32 = jnp.float32
BF16 = jnp.bfloat16
PARAMS = pltpu.CompilerParams(vmem_limit_bytes=20 * 1024 * 1024)
SMEM = pl.BlockSpec(memory_space=pltpu.SMEM)
ANY = pl.BlockSpec(memory_space=pl.ANY)
VMEM = pl.BlockSpec(memory_space=pltpu.VMEM)


def dot(lhs, rhs, lhs_dim, rhs_dim):
    return lax.dot_general(
        lhs, rhs, (((lhs_dim,), (rhs_dim,)), ((), ())), preferred_element_type=F32
    )


def halves(value, step):
    return value[:, step * 128 : (step + 1) * 128]


def start_kernel(win_ref, wout_ref, x_ref, shard_ref, copies_ref, sems):
    copies = [pltpu.make_async_copy(x_ref, copies_ref.at[q], sems.at[q]) for q in range(8)]
    for copy in copies:
        copy.start()
    rows = []
    for i in range(NB):
        w = win_ref[i].astype(F32)
        rows += [w[k : k + 1, c * 128 : (c + 1) * 128] for k in range(2) for c in range(4)]
    shard_ref[:48, :] = jnp.concatenate(rows).astype(BF16)
    shard_ref[48:, :] = wout_ref[...].astype(F32).reshape(48, 128).astype(BF16)
    for copy in copies:
        copy.wait()


def shard_rows(ref, rows):
    return jnp.concatenate([ref[:, 0, rows], ref[:, 1, rows]], axis=0).astype(F32)


def second_factor(first, mine_ref, other_ref, pair):
    rows = slice(48 + pair * 16, 48 + pair * 16 + 16)
    mine, other = shard_rows(mine_ref, rows), shard_rows(other_ref, rows)
    zero = jnp.where(first, mine, other)
    one = jnp.where(first, other, mine)
    return [
        jnp.stack([zero[:, cut], one[:, cut]], axis=1).reshape(512, 128).astype(BF16)
        for cut in (slice(0, 8), slice(8, 16))
    ]


def back_kernel(at_ref, mine_ref, other_ref, c_ref, send_ref, wide):
    first = at_ref[1] == 0
    for pair in range(NB // 2):
        for k, w in enumerate(second_factor(first, mine_ref, other_ref, pair)):
            o = pair * 2 + k
            d = dot(w, c_ref[:, o * 128 : (o + 1) * 128], 1, 1).reshape(8, 64, ROWS)
            for n in range(8):
                at = o * 512 + n * 64
                wide[at // 192, at % 192 : at % 192 + 64, :] = d[n]
    for p in range(8):
        for n in range(2):
            cut = slice(n * 128, n * 128 + 128)
            part = jnp.swapaxes(wide[:, p * 24 : (p + 1) * 24, cut], 0, 1)
            send_ref[p, :, :, cut] = part.astype(BF16)


def first_rows(ref, i):
    return jnp.swapaxes(shard_rows(ref, slice(i * 8, i * 8 + 8)), 0, 1)


def columns_kernel(mine_ref, send_ref):
    for pair in range(NB // 2):
        blocks = [first_rows(mine_ref, pair * 2), first_rows(mine_ref, pair * 2 + 1)]
        for c in range(4):
            rows = [blocks[i][k * 4 + c] for i in range(2) for k in range(2)]
            turned = jnp.concatenate(rows, axis=0).T.astype(BF16)
            for q in range(8):
                send_ref[q, pair, c * 16 : (c + 1) * 16, :] = turned[q * 16 : (q + 1) * 16]


ROOT = 0.7978845608028654


def first_grad_kernel(
    at_ref, mine_ref, other_ref, x_ref, back_ref, after_ref, gx_ref, keep_ref, send_ref
):
    first = at_ref[1] == 0
    row = lax.broadcasted_iota(jnp.int32, (128, 128), 0)
    col = lax.broadcasted_iota(jnp.int32, (128, 128), 1)
    pick = jnp.where(col == row % 32 * 4 + row // 32, 1.0, 0.0).astype(BF16)
    kept, sent = [], []
    for i in range(NB):
        mine, other = first_rows(mine_ref, i), first_rows(other_ref, i)
        zero, one = jnp.where(first, mine, other), jnp.where(first, other, mine)
        x = dot(pick, x_ref[:, i * 128 : (i + 1) * 128], 1, 1).astype(BF16)
        w = jnp.concatenate(
            [jnp.concatenate([zero[c], zero[4 + c], one[c], one[4 + c]]) for c in range(4)], axis=1
        ).astype(BF16)
        v = dot(w, x, 0, 0)
        square = v * v
        th = jnp.tanh(ROOT * (v + 0.044715 * (v * square)))
        slope = 0.5 * (1.0 + th) + (0.5 * ROOT) * v * (1.0 - th * th) * (1.0 + 0.134145 * square)
        back = jnp.concatenate([back_ref[:, i * 4 + c].reshape(128, ROWS) for c in range(4)])
        d = (back.astype(F32) * slope).astype(BF16)
        gx = dot(w, d, 1, 0)
        grad = dot(x, d, 1, 1).reshape(4, 32, 512)
        grads = [grad[:, :, c * 128 : (c + 1) * 128] for c in range(4)]
        gx_ref[:, i * 128 : (i + 1) * 128] = dot(gx.astype(BF16), pick, 0, 0).astype(BF16)
        by_core = [
            jnp.swapaxes(jnp.stack([grads[c][core * 2 + k] for k in range(2) for c in range(4)]), 0, 1)
            for core in range(2)
        ]
        kept.append(jnp.where(first, by_core[0], by_core[1]))
        sent.append(jnp.where(first, by_core[1], by_core[0]))
        if i % 2:
            rows = slice(i * 8 - 8, i * 8 + 8)
            keep_ref[:, rows, :] = jnp.concatenate(kept, axis=1).astype(BF16)
            send_ref[:, rows, :] = jnp.concatenate(sent, axis=1).astype(BF16)
            kept, sent = [], []


def second_grad_kernel(
    at_ref, x_ref, mine_ref, other_ref, c_ref, wmine_ref, wother_ref, out_ref, keep_ref,
    send_ref, mixed_ref, wide,
):
    first = at_ref[1] == 0
    row = lax.broadcasted_iota(jnp.int32, (256, 256), 0)
    col = lax.broadcasted_iota(jnp.int32, (256, 256), 1)
    target = (row // 64 % 2) * 128 + (row % 32) * 4 + (row // 128) * 2 + row // 32 % 2
    place = jnp.where(col == target, 1.0, 0.0).astype(BF16)
    for p in range(8):
        mine = mine_ref[p].reshape(192, 128).astype(F32)
        other = other_ref[p].reshape(192, 128).astype(F32)
        w = jnp.concatenate(
            [jnp.where(first, mine, other), jnp.where(first, other, mine)], axis=1
        ).astype(BF16)
        w = dot(w, place, 1, 0).astype(BF16)
        for i in range(NB):
            rows = slice(i // 2 * 64, i // 2 * 64 + 64)
            v = dot(
                w[rows, i % 2 * 128 : i % 2 * 128 + 128], x_ref[p, :, i * 128 : (i + 1) * 128], 1, 1
            )
            th = jnp.tanh(ROOT * (v + 0.044715 * (v * (v * v))))
            act = (0.5 * v) * (1.0 + th)
            start = (p * NB + i) * 4
            wide[start : start + 4] = act.reshape(4, 16, ROWS)
    for g in range(0, 192, 16):
        for n in range(2):
            cut = slice(n * 128, n * 128 + 128)
            part = jnp.swapaxes(wide[g : g + 16, :, cut], 0, 1).astype(BF16)
            for j in range(16):
                mixed_ref[j * 192 + g : j * 192 + g + 16, cut] = part[j]
    for pair in range(NB // 2):
        kept, sent = [], []
        wout = second_factor(first, wmine_ref, wother_ref, pair)
        for k in range(2):
            o = pair * 2 + k
            m = mixed_ref[o * 512 : (o + 1) * 512, :]
            out_ref[:, o * 128 : (o + 1) * 128] = dot(m, wout[k], 0, 0).astype(BF16)
            g = dot(m, c_ref[:, o * 128 : (o + 1) * 128], 1, 0).reshape(32, 2, 8, 128)
            kept.append(jnp.where(first, g[:, 0], g[:, 1]))
            sent.append(jnp.where(first, g[:, 1], g[:, 0]))
        rows = slice(pair * 16, pair * 16 + 16)
        keep_ref[:, rows, :] = jnp.concatenate(kept, axis=1).astype(BF16)
        send_ref[:, rows, :] = jnp.concatenate(sent, axis=1).astype(BF16)


def call(kernel, name, args, outs, scratch=(), unread=()):
    return pl.pallas_call(
        kernel,
        name=name,
        out_shape=[jax.ShapeDtypeStruct(shape, dtype) for shape, dtype in outs],
        in_specs=[
            ANY if n in unread else SMEM if arg.ndim == 1 else VMEM for n, arg in enumerate(args)
        ],
        out_specs=[VMEM] * len(outs),
        scratch_shapes=[pltpu.VMEM(shape, F32 if dtype is F32 else BF16) for shape, dtype in scratch],
        compiler_params=PARAMS,
        cost_estimate=pl.CostEstimate(
            flops=2 * 256 * 128 * 512 * 6, bytes_accessed=6_000_000, transcendentals=0
        ),
    )(*args)


def join_kernel(at_ref, keep_in, got_in, keep_out, got_out, both_ref):
    for n in range(32):
        place = lax.rem(n % RUN + RUN // 2 * at_ref[1], RUN)
        to = n // 16 * 16 + place * RUNS + n % 16 // RUN
        both_ref[to, :48, :] = (keep_in[n].astype(F32) + got_in[n].astype(F32)).astype(BF16)
        both_ref[to, 48:, :] = (keep_out[n].astype(F32) + got_out[n].astype(F32)).astype(BF16)


def part_kernel(got_ref, part_ref):
    total = got_ref[0].astype(F32)
    for n in range(1, 2 * RUN):
        total = total + got_ref[n].astype(F32)
    part_ref[...] = total.astype(BF16)


def total_kernel(got_ref, in_ref, out_ref):
    total = got_ref[0].astype(F32)
    for n in range(1, RUNS):
        total = total + got_ref[n].astype(F32)
    total = total * (1.0 / 128.0)
    out_ref[...] = total[48:].reshape(NB, 8, 128)
    for i in range(NB):
        for k in range(2):
            for c in range(4):
                row = i * 8 + k * 4 + c
                in_ref[i, k : k + 1, c * 128 : (c + 1) * 128] = total[row : row + 1]


RUN = 2
RUNS = 16 // RUN
NEAR = [
    [x * 32 + (run * RUN + RUN // 2 * core + n) % 16 * 2 + core for x in range(2) for n in range(RUN)]
    for core in range(2)
    for run in range(RUNS)
]
FAR = [
    [x * 32 + (run * RUN + n) * 2 + core for run in range(RUNS)]
    for x in range(2)
    for n in range(RUN)
    for core in range(2)
]


def exchange(value, axis, groups=None):
    return lax.all_to_all(value, axis, 0, 0, axis_index_groups=groups, tiled=True)


def swap_cores(value):
    return lax.ppermute(value, "core", [(0, 1), (1, 0)])


def on_device(tokens, w_in, w_out, cotangent):
    at = jnp.stack([lax.axis_index(MP), lax.axis_index("core")]).astype(jnp.int32)
    shard, copies = pl.pallas_call(
        start_kernel,
        name="start",
        out_shape=[
            jax.ShapeDtypeStruct((96, 128), BF16),
            jax.ShapeDtypeStruct((8, ROWS, 768), BF16),
        ],
        in_specs=[VMEM, VMEM, VMEM],
        out_specs=[VMEM, ANY],
        scratch_shapes=[pltpu.SemaphoreType.DMA((8,))],
        compiler_params=pltpu.CompilerParams(vmem_limit_bytes=62 * 1024 * 1024),
    )(w_in.transpose(1, 0, 2), w_out.transpose(1, 0, 2), tokens)
    pair = lax.all_gather(shard, "x_hi", axis=0, tiled=False)
    copies, pair = lax.optimization_barrier((copies, pair))
    gathered = exchange(copies, MP)
    mine = lax.all_gather(pair, "z", axis=0, tiled=False)
    other = swap_cores(mine)

    half = ((32, 48, 128), BF16)
    (column_send,) = call(
        columns_kernel, "columns", (mine,), [((8, 3, 64, 128), BF16)]
    )
    column_send, gathered = lax.optimization_barrier((column_send, gathered))
    columns = exchange(column_send, MP)
    other_columns = swap_cores(columns)
    (back_send,) = call(
        back_kernel, "d_mixed", (at, mine, other, cotangent),
        [((8, 24, 16, ROWS), BF16)], [((16, 192, ROWS), F32)],
    )
    back = exchange(back_send, MP)
    output, keep_out, send_out = call(
        second_grad_kernel, "second_grad",
        (at, gathered, columns, other_columns, cotangent, mine, other),
        [((ROWS, 768), BF16), half, half],
        [((3072, ROWS), BF16), ((192, 16, ROWS), F32)],
    )
    got_out = swap_cores(send_out)
    grad_tokens, keep_in, send_in = call(
        first_grad_kernel, "first_grad", (at, mine, other, tokens, back, got_out),
        [((ROWS, 768), BF16), half, half], (), (5,),
    )
    got_in = swap_cores(send_in)
    (both,) = call(
        join_kernel, "join", (at, keep_in, got_in, keep_out, got_out), [((32, 96, 128), BF16)]
    )
    near = exchange(both.reshape(2 * RUN, RUNS, 96, 128), DP, NEAR)
    (part,) = call(part_kernel, "part", (near,), [((RUNS, 96, 128), BF16)])
    grad_in, grad_out = call(
        total_kernel, "total", (exchange(part, DP, FAR),),
        [((NB, 2, 512), F32), ((NB, 8, 128), F32)],
    )
    grad_in, grad_out = grad_in.transpose(1, 0, 2), grad_out.transpose(1, 0, 2)
    return (output, grad_tokens, grad_in, grad_out)


def solution(mesh):
    fine = Mesh(mesh.devices.reshape(SIZES), DP + MP)
    placed = (P(DP, MP), P(DP, MP, None), P(DP, MP, None), P(DP, MP))
    return jax.shard_map(
        on_device,
        mesh=fine,
        in_specs=placed,
        out_specs=(P(DP, MP), P(DP, MP), P(DP, MP, None), P(DP, MP, None)),
        check_vma=False,
    )
```

```python
import jax
import jax.numpy as jnp
from jax import lax
from jax.experimental import pallas as pl
from jax.experimental.pallas import tpu as pltpu
from jax.sharding import Mesh, PartitionSpec as P

NB = 6
ROWS = 256
DP = ("x_hi", "z", "core")
MP = ("x_lo", "y")
SIZES = (2, 16, 2, 2, 4)
F32 = jnp.float32
BF16 = jnp.bfloat16
PARAMS = pltpu.CompilerParams(vmem_limit_bytes=20 * 1024 * 1024)
SMEM = pl.BlockSpec(memory_space=pltpu.SMEM)
ANY = pl.BlockSpec(memory_space=pl.ANY)
VMEM = pl.BlockSpec(memory_space=pltpu.VMEM)


def dot(lhs, rhs, lhs_dim, rhs_dim):
    return lax.dot_general(
        lhs, rhs, (((lhs_dim,), (rhs_dim,)), ((), ())), preferred_element_type=F32
    )


def halves(value, step):
    return value[:, step * 128 : (step + 1) * 128]


def start_kernel(win_ref, wout_ref, x_ref, shard_ref, copies_ref, sems):
    copies = [pltpu.make_async_copy(x_ref, copies_ref.at[q], sems.at[q]) for q in range(8)]
    for copy in copies:
        copy.start()
    rows = []
    for i in range(NB):
        w = win_ref[i].astype(F32)
        rows += [w[k : k + 1, c * 128 : (c + 1) * 128] for k in range(2) for c in range(4)]
    shard_ref[:48, :] = jnp.concatenate(rows).astype(BF16)
    shard_ref[48:, :] = wout_ref[...].astype(F32).reshape(48, 128).astype(BF16)
    for copy in copies:
        copy.wait()


def shard_rows(ref, rows):
    return jnp.concatenate([ref[:, 0, rows], ref[:, 1, rows]], axis=0).astype(F32)


def second_factor(first, mine_ref, other_ref, pair):
    rows = slice(48 + pair * 16, 48 + pair * 16 + 16)
    mine, other = shard_rows(mine_ref, rows), shard_rows(other_ref, rows)
    zero = jnp.where(first, mine, other)
    one = jnp.where(first, other, mine)
    return [
        jnp.stack([zero[:, cut], one[:, cut]], axis=1).reshape(512, 128).astype(BF16)
        for cut in (slice(0, 8), slice(8, 16))
    ]


def back_kernel(at_ref, mine_ref, other_ref, c_ref, send_ref, wide):
    first = at_ref[1] == 0
    for pair in range(NB // 2):
        for k, w in enumerate(second_factor(first, mine_ref, other_ref, pair)):
            o = pair * 2 + k
            d = dot(w, c_ref[:, o * 128 : (o + 1) * 128], 1, 1).reshape(8, 64, ROWS)
            for n in range(8):
                at = o * 512 + n * 64
                wide[at // 192, at % 192 : at % 192 + 64, :] = d[n]
    for p in range(8):
        for n in range(2):
            cut = slice(n * 128, n * 128 + 128)
            part = jnp.swapaxes(wide[:, p * 24 : (p + 1) * 24, cut], 0, 1)
            send_ref[p, :, :, cut] = part.astype(BF16)


def first_rows(ref, i):
    both = shard_rows(ref, slice(i // 2 * 16, i // 2 * 16 + 16))
    return jnp.swapaxes(both[:, i % 2 * 8 : i % 2 * 8 + 8], 0, 1)


def columns_kernel(mine_ref, send_ref):
    for pair in range(NB // 2):
        blocks = [first_rows(mine_ref, pair * 2), first_rows(mine_ref, pair * 2 + 1)]
        for c in range(4):
            rows = [blocks[i][k * 4 + c] for i in range(2) for k in range(2)]
            turned = jnp.concatenate(rows, axis=0).T.astype(BF16)
            for q in range(8):
                send_ref[q, pair, c * 16 : (c + 1) * 16, :] = turned[q * 16 : (q + 1) * 16]


ROOT = 0.7978845608028654


def first_grad_kernel(
    at_ref, mine_ref, other_ref, x_ref, back_ref, after_ref, gx_ref, keep_ref, send_ref
):
    first = at_ref[1] == 0
    row = lax.broadcasted_iota(jnp.int32, (128, 128), 0)
    col = lax.broadcasted_iota(jnp.int32, (128, 128), 1)
    pick = jnp.where(col == row % 32 * 4 + row // 32, 1.0, 0.0).astype(BF16)
    kept, sent = [], []
    for i in range(NB):
        mine, other = first_rows(mine_ref, i), first_rows(other_ref, i)
        zero, one = jnp.where(first, mine, other), jnp.where(first, other, mine)
        x = dot(pick, x_ref[:, i * 128 : (i + 1) * 128], 1, 1).astype(BF16)
        w = jnp.concatenate(
            [jnp.concatenate([zero[c], zero[4 + c], one[c], one[4 + c]]) for c in range(4)], axis=1
        ).astype(BF16)
        v = dot(w, x, 0, 0)
        square = v * v
        th = jnp.tanh(ROOT * (v + 0.044715 * (v * square)))
        slope = 0.5 * (1.0 + th) + (0.5 * ROOT) * v * (1.0 - th * th) * (1.0 + 0.134145 * square)
        back = jnp.concatenate([back_ref[:, i * 4 + c].reshape(128, ROWS) for c in range(4)])
        d = (back.astype(F32) * slope).astype(BF16)
        gx = dot(w, d, 1, 0)
        grad = dot(x, d, 1, 1).reshape(4, 32, 512)
        grads = [grad[:, :, c * 128 : (c + 1) * 128] for c in range(4)]
        gx_ref[:, i * 128 : (i + 1) * 128] = dot(gx.astype(BF16), pick, 0, 0).astype(BF16)
        by_core = [
            jnp.swapaxes(jnp.stack([grads[c][core * 2 + k] for k in range(2) for c in range(4)]), 0, 1)
            for core in range(2)
        ]
        kept.append(jnp.where(first, by_core[0], by_core[1]))
        sent.append(jnp.where(first, by_core[1], by_core[0]))
        if i % 2:
            rows = slice(i * 8 - 8, i * 8 + 8)
            keep_ref[:, rows, :] = jnp.concatenate(kept, axis=1).astype(BF16)
            send_ref[:, rows, :] = jnp.concatenate(sent, axis=1).astype(BF16)
            kept, sent = [], []


def second_grad_kernel(
    at_ref, x_ref, mine_ref, other_ref, c_ref, wmine_ref, wother_ref, out_ref, keep_ref,
    send_ref, mixed_ref, wide,
):
    first = at_ref[1] == 0
    row = lax.broadcasted_iota(jnp.int32, (256, 256), 0)
    col = lax.broadcasted_iota(jnp.int32, (256, 256), 1)
    target = (row // 64 % 2) * 128 + (row % 32) * 4 + (row // 128) * 2 + row // 32 % 2
    place = jnp.where(col == target, 1.0, 0.0).astype(BF16)
    for p in range(8):
        mine = mine_ref[p].reshape(192, 128).astype(F32)
        other = other_ref[p].reshape(192, 128).astype(F32)
        w = jnp.concatenate(
            [jnp.where(first, mine, other), jnp.where(first, other, mine)], axis=1
        ).astype(BF16)
        w = dot(w, place, 1, 0).astype(BF16)
        for i in range(NB):
            rows = slice(i // 2 * 64, i // 2 * 64 + 64)
            v = dot(
                w[rows, i % 2 * 128 : i % 2 * 128 + 128], x_ref[p, :, i * 128 : (i + 1) * 128], 1, 1
            )
            th = jnp.tanh(ROOT * (v + 0.044715 * (v * (v * v))))
            act = (0.5 * v) * (1.0 + th)
            start = (p * NB + i) * 4
            wide[start : start + 4] = act.reshape(4, 16, ROWS)
    for g in range(0, 192, 16):
        for n in range(2):
            cut = slice(n * 128, n * 128 + 128)
            part = jnp.swapaxes(wide[g : g + 16, :, cut], 0, 1).astype(BF16)
            for j in range(16):
                mixed_ref[j * 192 + g : j * 192 + g + 16, cut] = part[j]
    for pair in range(NB // 2):
        kept, sent = [], []
        wout = second_factor(first, wmine_ref, wother_ref, pair)
        for k in range(2):
            o = pair * 2 + k
            m = mixed_ref[o * 512 : (o + 1) * 512, :]
            out_ref[:, o * 128 : (o + 1) * 128] = dot(m, wout[k], 0, 0).astype(BF16)
            g = dot(m, c_ref[:, o * 128 : (o + 1) * 128], 1, 0).reshape(32, 2, 8, 128)
            kept.append(jnp.where(first, g[:, 0], g[:, 1]))
            sent.append(jnp.where(first, g[:, 1], g[:, 0]))
        rows = slice(pair * 16, pair * 16 + 16)
        keep_ref[:, rows, :] = jnp.concatenate(kept, axis=1).astype(BF16)
        send_ref[:, rows, :] = jnp.concatenate(sent, axis=1).astype(BF16)


def call(kernel, name, args, outs, scratch=(), unread=()):
    return pl.pallas_call(
        kernel,
        name=name,
        out_shape=[jax.ShapeDtypeStruct(shape, dtype) for shape, dtype in outs],
        in_specs=[
            ANY if n in unread else SMEM if arg.ndim == 1 else VMEM for n, arg in enumerate(args)
        ],
        out_specs=[VMEM] * len(outs),
        scratch_shapes=[pltpu.VMEM(shape, F32 if dtype is F32 else BF16) for shape, dtype in scratch],
        compiler_params=PARAMS,
        cost_estimate=pl.CostEstimate(
            flops=2 * 256 * 128 * 512 * 6, bytes_accessed=6_000_000, transcendentals=0
        ),
    )(*args)


def join_kernel(at_ref, keep_in, got_in, keep_out, got_out, both_ref):
    for n in range(32):
        place = lax.rem(n % RUN + RUN // 2 * at_ref[1], RUN)
        to = n // 16 * 16 + place * RUNS + n % 16 // RUN
        both_ref[to, :48, :] = (keep_in[n].astype(F32) + got_in[n].astype(F32)).astype(BF16)
        both_ref[to, 48:, :] = (keep_out[n].astype(F32) + got_out[n].astype(F32)).astype(BF16)


def part_kernel(got_ref, part_ref):
    total = got_ref[0].astype(F32)
    for n in range(1, 2 * RUN):
        total = total + got_ref[n].astype(F32)
    part_ref[...] = total.astype(BF16)


def total_kernel(got_ref, in_ref, out_ref):
    total = got_ref[0].astype(F32)
    for n in range(1, RUNS):
        total = total + got_ref[n].astype(F32)
    total = total * (1.0 / 128.0)
    out_ref[...] = total[48:].reshape(NB, 8, 128)
    for i in range(NB):
        for k in range(2):
            for c in range(4):
                row = i * 8 + k * 4 + c
                in_ref[i, k : k + 1, c * 128 : (c + 1) * 128] = total[row : row + 1]


RUN = 2
RUNS = 16 // RUN
NEAR = [
    [x * 32 + (run * RUN + RUN // 2 * core + n) % 16 * 2 + core for x in range(2) for n in range(RUN)]
    for core in range(2)
    for run in range(RUNS)
]
FAR = [
    [x * 32 + (run * RUN + n) * 2 + core for run in range(RUNS)]
    for x in range(2)
    for n in range(RUN)
    for core in range(2)
]


def exchange(value, axis, groups=None):
    return lax.all_to_all(value, axis, 0, 0, axis_index_groups=groups, tiled=True)


def swap_cores(value):
    return lax.ppermute(value, "core", [(0, 1), (1, 0)])


def on_device(tokens, w_in, w_out, cotangent):
    at = jnp.stack([lax.axis_index(MP), lax.axis_index("core")]).astype(jnp.int32)
    shard, copies = pl.pallas_call(
        start_kernel,
        name="start",
        out_shape=[
            jax.ShapeDtypeStruct((96, 128), BF16),
            jax.ShapeDtypeStruct((8, ROWS, 768), BF16),
        ],
        in_specs=[VMEM, VMEM, VMEM],
        out_specs=[VMEM, ANY],
        scratch_shapes=[pltpu.SemaphoreType.DMA((8,))],
        compiler_params=pltpu.CompilerParams(vmem_limit_bytes=62 * 1024 * 1024),
    )(w_in.transpose(1, 0, 2), w_out.transpose(1, 0, 2), tokens)
    pair = lax.all_gather(shard, "x_hi", axis=0, tiled=False)
    copies, pair = lax.optimization_barrier((copies, pair))
    gathered = exchange(copies, MP)
    mine = lax.all_gather(pair, "z", axis=0, tiled=False)
    other = swap_cores(mine)

    half = ((32, 48, 128), BF16)
    (column_send,) = call(
        columns_kernel, "columns", (mine,), [((8, 3, 64, 128), BF16)]
    )
    column_send, gathered = lax.optimization_barrier((column_send, gathered))
    columns = exchange(column_send, MP)
    other_columns = swap_cores(columns)
    (back_send,) = call(
        back_kernel, "d_mixed", (at, mine, other, cotangent),
        [((8, 24, 16, ROWS), BF16)], [((16, 192, ROWS), F32)],
    )
    back = exchange(back_send, MP)
    output, keep_out, send_out = call(
        second_grad_kernel, "second_grad",
        (at, gathered, columns, other_columns, cotangent, mine, other),
        [((ROWS, 768), BF16), half, half],
        [((3072, ROWS), BF16), ((192, 16, ROWS), F32)],
    )
    got_out = swap_cores(send_out)
    grad_tokens, keep_in, send_in = call(
        first_grad_kernel, "first_grad", (at, mine, other, tokens, back, got_out),
        [((ROWS, 768), BF16), half, half], (), (5,),
    )
    got_in = swap_cores(send_in)
    (both,) = call(
        join_kernel, "join", (at, keep_in, got_in, keep_out, got_out), [((32, 96, 128), BF16)]
    )
    near = exchange(both.reshape(2 * RUN, RUNS, 96, 128), DP, NEAR)
    (part,) = call(part_kernel, "part", (near,), [((RUNS, 96, 128), BF16)])
    grad_in, grad_out = call(
        total_kernel, "total", (exchange(part, DP, FAR),),
        [((NB, 2, 512), F32), ((NB, 8, 128), F32)],
    )
    grad_in, grad_out = grad_in.transpose(1, 0, 2), grad_out.transpose(1, 0, 2)
    return (output, grad_tokens, grad_in, grad_out)


def solution(mesh):
    fine = Mesh(mesh.devices.reshape(SIZES), DP + MP)
    placed = (P(DP, MP), P(DP, MP, None), P(DP, MP, None), P(DP, MP))
    return jax.shard_map(
        on_device,
        mesh=fine,
        in_specs=placed,
        out_specs=(P(DP, MP), P(DP, MP), P(DP, MP, None), P(DP, MP, None)),
        check_vma=False,
    )
```

```python
import jax
import jax.numpy as jnp
from jax import lax
from jax.experimental import pallas as pl
from jax.experimental.pallas import tpu as pltpu
from jax.sharding import Mesh, PartitionSpec as P

NB = 6
ROWS = 256
DP = ("x_hi", "z", "core")
MP = ("x_lo", "y")
SIZES = (2, 16, 2, 2, 4)
F32 = jnp.float32
BF16 = jnp.bfloat16
PARAMS = pltpu.CompilerParams(vmem_limit_bytes=20 * 1024 * 1024)
SMEM = pl.BlockSpec(memory_space=pltpu.SMEM)
ANY = pl.BlockSpec(memory_space=pl.ANY)
VMEM = pl.BlockSpec(memory_space=pltpu.VMEM)


def dot(lhs, rhs, lhs_dim, rhs_dim):
    return lax.dot_general(
        lhs, rhs, (((lhs_dim,), (rhs_dim,)), ((), ())), preferred_element_type=F32
    )


def halves(value, step):
    return value[:, step * 128 : (step + 1) * 128]


def start_kernel(win_ref, wout_ref, x_ref, shard_ref, copies_ref, sems):
    copies = [pltpu.make_async_copy(x_ref, copies_ref.at[q], sems.at[q]) for q in range(8)]
    for copy in copies:
        copy.start()
    rows = []
    for i in range(NB):
        w = win_ref[i].astype(F32)
        rows += [w[k : k + 1, c * 128 : (c + 1) * 128] for k in range(2) for c in range(4)]
    shard_ref[:48, :] = jnp.concatenate(rows).astype(BF16)
    shard_ref[48:, :] = wout_ref[...].astype(F32).reshape(48, 128).astype(BF16)
    for copy in copies:
        copy.wait()


def shard_rows(ref, rows):
    return jnp.concatenate([ref[:, 0, rows], ref[:, 1, rows]], axis=0).astype(F32)


def second_factor(first, mine_ref, other_ref, pair):
    rows = slice(48 + pair * 16, 48 + pair * 16 + 16)
    mine, other = shard_rows(mine_ref, rows), shard_rows(other_ref, rows)
    zero = jnp.where(first, mine, other)
    one = jnp.where(first, other, mine)
    return [
        jnp.stack([zero[:, cut], one[:, cut]], axis=1).reshape(512, 128).astype(BF16)
        for cut in (slice(0, 8), slice(8, 16))
    ]


def back_kernel(at_ref, mine_ref, other_ref, c_ref, send_ref, wide):
    first = at_ref[1] == 0
    for pair in range(NB // 2):
        for k, w in enumerate(second_factor(first, mine_ref, other_ref, pair)):
            o = pair * 2 + k
            d = dot(w, c_ref[:, o * 128 : (o + 1) * 128], 1, 1).reshape(8, 64, ROWS)
            for n in range(8):
                at = o * 512 + n * 64
                wide[at // 192, at % 192 : at % 192 + 64, :] = d[n]
    for p in range(8):
        for n in range(2):
            cut = slice(n * 128, n * 128 + 128)
            part = jnp.swapaxes(wide[:, p * 24 : (p + 1) * 24, cut], 0, 1)
            send_ref[p, :, :, cut] = part.astype(BF16)


def first_rows(ref, i):
    both = shard_rows(ref, slice(i // 2 * 16, i // 2 * 16 + 16))
    return jnp.swapaxes(both[:, i % 2 * 8 : i % 2 * 8 + 8], 0, 1)


def columns_kernel(mine_ref, send_ref):
    for pair in range(NB // 2):
        blocks = [first_rows(mine_ref, pair * 2), first_rows(mine_ref, pair * 2 + 1)]
        for c in range(4):
            rows = [blocks[i][k * 4 + c] for i in range(2) for k in range(2)]
            turned = jnp.concatenate(rows, axis=0).T.astype(BF16)
            for q in range(8):
                send_ref[q, pair, c * 16 : (c + 1) * 16, :] = turned[q * 16 : (q + 1) * 16]


ROOT = 0.7978845608028654


def first_grad_kernel(
    at_ref, mine_ref, other_ref, x_ref, back_ref, after_ref, gx_ref, keep_ref, send_ref
):
    first = at_ref[1] == 0
    row = lax.broadcasted_iota(jnp.int32, (128, 128), 0)
    col = lax.broadcasted_iota(jnp.int32, (128, 128), 1)
    pick = jnp.where(col == row % 32 * 4 + row // 32, 1.0, 0.0).astype(BF16)
    kept, sent = [], []
    for i in range(NB):
        mine, other = first_rows(mine_ref, i), first_rows(other_ref, i)
        zero, one = jnp.where(first, mine, other), jnp.where(first, other, mine)
        x = dot(pick, x_ref[:, i * 128 : (i + 1) * 128], 1, 1).astype(BF16)
        w = jnp.concatenate(
            [jnp.concatenate([zero[c], zero[4 + c], one[c], one[4 + c]]) for c in range(4)], axis=1
        ).astype(BF16)
        v = dot(w, x, 0, 0)
        square = v * v
        th = jnp.tanh(ROOT * (v + 0.044715 * (v * square)))
        slope = 0.5 * (1.0 + th) + (0.5 * ROOT) * v * (1.0 - th * th) * (1.0 + 0.134145 * square)
        back = jnp.concatenate([back_ref[:, i * 4 + c].reshape(128, ROWS) for c in range(4)])
        d = (back.astype(F32) * slope).astype(BF16)
        gx = dot(w, d, 1, 0)
        grad = dot(x, d, 1, 1).reshape(4, 32, 512)
        grads = [grad[:, :, c * 128 : (c + 1) * 128] for c in range(4)]
        gx_ref[:, i * 128 : (i + 1) * 128] = dot(gx.astype(BF16), pick, 0, 0).astype(BF16)
        by_core = [
            jnp.swapaxes(jnp.stack([grads[c][core * 2 + k] for k in range(2) for c in range(4)]), 0, 1)
            for core in range(2)
        ]
        kept.append(jnp.where(first, by_core[0], by_core[1]))
        sent.append(jnp.where(first, by_core[1], by_core[0]))
        if i % 2:
            rows = slice(i * 8 - 8, i * 8 + 8)
            keep_ref[:, rows, :] = jnp.concatenate(kept, axis=1).astype(BF16)
            send_ref[:, rows, :] = jnp.concatenate(sent, axis=1).astype(BF16)
            kept, sent = [], []


def second_grad_kernel(
    at_ref, x_ref, mine_ref, other_ref, c_ref, wmine_ref, wother_ref, out_ref, keep_ref,
    send_ref, mixed_ref, wide,
):
    first = at_ref[1] == 0
    row = lax.broadcasted_iota(jnp.int32, (256, 256), 0)
    col = lax.broadcasted_iota(jnp.int32, (256, 256), 1)
    target = (row // 64 % 2) * 128 + (row % 32) * 4 + (row // 128) * 2 + row // 32 % 2
    place = jnp.where(col == target, 1.0, 0.0).astype(BF16)
    for p in range(8):
        mine = mine_ref[p].reshape(192, 128).astype(F32)
        other = other_ref[p].reshape(192, 128).astype(F32)
        w = jnp.concatenate(
            [jnp.where(first, mine, other), jnp.where(first, other, mine)], axis=1
        ).astype(BF16)
        w = dot(w, place, 1, 0).astype(BF16)
        for i in range(NB):
            rows = slice(i // 2 * 64, i // 2 * 64 + 64)
            v = dot(
                w[rows, i % 2 * 128 : i % 2 * 128 + 128], x_ref[p, :, i * 128 : (i + 1) * 128], 1, 1
            )
            th = jnp.tanh(ROOT * (v + 0.044715 * (v * (v * v))))
            act = (0.5 * v) * (1.0 + th)
            start = (p * NB + i) * 4
            wide[start : start + 4] = act.reshape(4, 16, ROWS)
    for g in range(0, 192, 16):
        for n in range(2):
            cut = slice(n * 128, n * 128 + 128)
            part = jnp.swapaxes(wide[g : g + 16, :, cut], 0, 1).astype(BF16)
            for j in range(16):
                mixed_ref[j * 192 + g : j * 192 + g + 16, cut] = part[j]
    for pair in range(NB // 2):
        kept, sent = [], []
        wout = second_factor(first, wmine_ref, wother_ref, pair)
        for k in range(2):
            o = pair * 2 + k
            m = mixed_ref[o * 512 : (o + 1) * 512, :]
            out_ref[:, o * 128 : (o + 1) * 128] = dot(m, wout[k], 0, 0).astype(BF16)
            g = dot(m, c_ref[:, o * 128 : (o + 1) * 128], 1, 0).reshape(32, 2, 8, 128)
            kept.append(jnp.where(first, g[:, 0], g[:, 1]))
            sent.append(jnp.where(first, g[:, 1], g[:, 0]))
        rows = slice(pair * 16, pair * 16 + 16)
        keep_ref[:, rows, :] = jnp.concatenate(kept, axis=1).astype(BF16)
        send_ref[:, rows, :] = jnp.concatenate(sent, axis=1).astype(BF16)


def call(kernel, name, args, outs, scratch=(), unread=()):
    return pl.pallas_call(
        kernel,
        name=name,
        out_shape=[jax.ShapeDtypeStruct(shape, dtype) for shape, dtype in outs],
        in_specs=[
            ANY if n in unread else SMEM if arg.ndim == 1 else VMEM for n, arg in enumerate(args)
        ],
        out_specs=[VMEM] * len(outs),
        scratch_shapes=[pltpu.VMEM(shape, F32 if dtype is F32 else BF16) for shape, dtype in scratch],
        compiler_params=PARAMS,
        cost_estimate=pl.CostEstimate(
            flops=2 * 256 * 128 * 512 * 6, bytes_accessed=6_000_000, transcendentals=0
        ),
    )(*args)


def join_kernel(at_ref, keep_in, got_in, keep_out, got_out, both_ref):
    for n in range(32):
        place = lax.rem(n % RUN + RUN // 2 * at_ref[1], RUN)
        turn = RUNS // 2 * at_ref[1] + RUNS // 4 * (n % RUN)
        run = lax.rem(n % 16 // RUN + 2 * RUNS - turn, RUNS)
        to = lax.rem(n // 16 + at_ref[1], 2) * 16 + place * RUNS + run
        both_ref[to, :48, :] = (keep_in[n].astype(F32) + got_in[n].astype(F32)).astype(BF16)
        both_ref[to, 48:, :] = (keep_out[n].astype(F32) + got_out[n].astype(F32)).astype(BF16)


def part_kernel(got_ref, part_ref):
    total = got_ref[0].astype(F32)
    for n in range(1, 2 * RUN):
        total = total + got_ref[n].astype(F32)
    part_ref[...] = total.astype(BF16)


def total_kernel(got_ref, in_ref, out_ref):
    total = got_ref[0].astype(F32)
    for n in range(1, RUNS):
        total = total + got_ref[n].astype(F32)
    total = total * (1.0 / 128.0)
    out_ref[...] = total[48:].reshape(NB, 8, 128)
    for i in range(NB):
        for k in range(2):
            for c in range(4):
                row = i * 8 + k * 4 + c
                in_ref[i, k : k + 1, c * 128 : (c + 1) * 128] = total[row : row + 1]


RUN = 2
RUNS = 16 // RUN
NEAR = [
    [x * 32 + (run * RUN + RUN // 2 * core + n) % 16 * 2 + core for x in (core, 1 - core) for n in range(RUN)]
    for core in range(2)
    for run in range(RUNS)
]
FAR = [
    [
        x * 32 + ((run + RUNS // 2 * core + RUNS // 4 * n) % RUNS * RUN + n) * 2 + core
        for run in range(RUNS)
    ]
    for x in range(2)
    for n in range(RUN)
    for core in range(2)
]


def exchange(value, axis, groups=None):
    return lax.all_to_all(value, axis, 0, 0, axis_index_groups=groups, tiled=True)


def swap_cores(value):
    return lax.ppermute(value, "core", [(0, 1), (1, 0)])


def on_device(tokens, w_in, w_out, cotangent):
    at = jnp.stack([lax.axis_index(MP), lax.axis_index("core")]).astype(jnp.int32)
    shard, copies = pl.pallas_call(
        start_kernel,
        name="start",
        out_shape=[
            jax.ShapeDtypeStruct((96, 128), BF16),
            jax.ShapeDtypeStruct((8, ROWS, 768), BF16),
        ],
        in_specs=[VMEM, VMEM, VMEM],
        out_specs=[VMEM, ANY],
        scratch_shapes=[pltpu.SemaphoreType.DMA((8,))],
        compiler_params=pltpu.CompilerParams(vmem_limit_bytes=62 * 1024 * 1024),
    )(w_in.transpose(1, 0, 2), w_out.transpose(1, 0, 2), tokens)
    pair = lax.all_gather(shard, "x_hi", axis=0, tiled=False)
    copies, pair = lax.optimization_barrier((copies, pair))
    gathered = exchange(copies, MP)
    mine = lax.all_gather(pair, "z", axis=0, tiled=False)
    other = swap_cores(mine)

    half = ((32, 48, 128), BF16)
    (column_send,) = call(
        columns_kernel, "columns", (mine,), [((8, 3, 64, 128), BF16)]
    )
    column_send, gathered = lax.optimization_barrier((column_send, gathered))
    columns = exchange(column_send, MP)
    other_columns = swap_cores(columns)
    (back_send,) = call(
        back_kernel, "d_mixed", (at, mine, other, cotangent),
        [((8, 24, 16, ROWS), BF16)], [((16, 192, ROWS), F32)],
    )
    back = exchange(back_send, MP)
    output, keep_out, send_out = call(
        second_grad_kernel, "second_grad",
        (at, gathered, columns, other_columns, cotangent, mine, other),
        [((ROWS, 768), BF16), half, half],
        [((3072, ROWS), BF16), ((192, 16, ROWS), F32)],
    )
    got_out = swap_cores(send_out)
    grad_tokens, keep_in, send_in = call(
        first_grad_kernel, "first_grad", (at, mine, other, tokens, back, got_out),
        [((ROWS, 768), BF16), half, half], (), (5,),
    )
    got_in = swap_cores(send_in)
    (both,) = call(
        join_kernel, "join", (at, keep_in, got_in, keep_out, got_out), [((32, 96, 128), BF16)]
    )
    near = exchange(both.reshape(2 * RUN, RUNS, 96, 128), DP, NEAR)
    (part,) = call(part_kernel, "part", (near,), [((RUNS, 96, 128), BF16)])
    grad_in, grad_out = call(
        total_kernel, "total", (exchange(part, DP, FAR),),
        [((NB, 2, 512), F32), ((NB, 8, 128), F32)],
    )
    grad_in, grad_out = grad_in.transpose(1, 0, 2), grad_out.transpose(1, 0, 2)
    return (output, grad_tokens, grad_in, grad_out)


def solution(mesh):
    fine = Mesh(mesh.devices.reshape(SIZES), DP + MP)
    placed = (P(DP, MP), P(DP, MP, None), P(DP, MP, None), P(DP, MP))
    return jax.shard_map(
        on_device,
        mesh=fine,
        in_specs=placed,
        out_specs=(P(DP, MP), P(DP, MP), P(DP, MP, None), P(DP, MP, None)),
        check_vma=False,
    )
```

```python
import jax
import jax.numpy as jnp
from jax import lax
from jax.experimental import pallas as pl
from jax.experimental.pallas import tpu as pltpu
from jax.sharding import Mesh, PartitionSpec as P

NB = 6
ROWS = 256
DP = ("x_hi", "z", "core")
MP = ("x_lo", "y")
SIZES = (2, 16, 2, 2, 4)
F32 = jnp.float32
BF16 = jnp.bfloat16
PARAMS = pltpu.CompilerParams(vmem_limit_bytes=20 * 1024 * 1024)
SMEM = pl.BlockSpec(memory_space=pltpu.SMEM)
ANY = pl.BlockSpec(memory_space=pl.ANY)
VMEM = pl.BlockSpec(memory_space=pltpu.VMEM)


def dot(lhs, rhs, lhs_dim, rhs_dim):
    return lax.dot_general(
        lhs, rhs, (((lhs_dim,), (rhs_dim,)), ((), ())), preferred_element_type=F32
    )


def halves(value, step):
    return value[:, step * 128 : (step + 1) * 128]


def start_kernel(win_ref, wout_ref, x_ref, shard_ref, copies_ref, sems):
    copies = [pltpu.make_async_copy(x_ref, copies_ref.at[q], sems.at[q]) for q in range(8)]
    for copy in copies:
        copy.start()
    rows = []
    for i in range(NB):
        w = win_ref[i].astype(F32)
        rows += [w[k : k + 1, c * 128 : (c + 1) * 128] for k in range(2) for c in range(4)]
    shard_ref[:48, :] = jnp.concatenate(rows).astype(BF16)
    shard_ref[48:, :] = wout_ref[...].astype(F32).reshape(48, 128).astype(BF16)
    for copy in copies:
        copy.wait()


def shard_rows(ref, rows):
    return jnp.concatenate([ref[:, 0, rows], ref[:, 1, rows]], axis=0).astype(F32)


def second_factor(first, mine_ref, other_ref, pair):
    rows = slice(48 + pair * 16, 48 + pair * 16 + 16)
    mine, other = shard_rows(mine_ref, rows), shard_rows(other_ref, rows)
    zero = jnp.where(first, mine, other)
    one = jnp.where(first, other, mine)
    return [
        jnp.stack([zero[:, cut], one[:, cut]], axis=1).reshape(512, 128).astype(BF16)
        for cut in (slice(0, 8), slice(8, 16))
    ]


def back_kernel(at_ref, mine_ref, other_ref, c_ref, send_ref, wide):
    first = at_ref[1] == 0
    for pair in range(NB // 2):
        for k, w in enumerate(second_factor(first, mine_ref, other_ref, pair)):
            o = pair * 2 + k
            d = dot(w, c_ref[:, o * 128 : (o + 1) * 128], 1, 1).reshape(8, 64, ROWS)
            for n in range(8):
                at = o * 512 + n * 64
                wide[at // 192, at % 192 : at % 192 + 64, :] = d[n]
    for p in range(8):
        for n in range(2):
            cut = slice(n * 128, n * 128 + 128)
            part = jnp.swapaxes(wide[:, p * 24 : (p + 1) * 24, cut], 0, 1)
            send_ref[p, :, :, cut] = part.astype(BF16)


def first_rows(ref, i):
    both = shard_rows(ref, slice(i // 2 * 16, i // 2 * 16 + 16))
    return jnp.swapaxes(both[:, i % 2 * 8 : i % 2 * 8 + 8], 0, 1)


def columns_kernel(mine_ref, send_ref):
    for pair in range(NB // 2):
        blocks = [first_rows(mine_ref, pair * 2), first_rows(mine_ref, pair * 2 + 1)]
        for c in range(4):
            rows = [blocks[i][k * 4 + c] for i in range(2) for k in range(2)]
            turned = jnp.concatenate(rows, axis=0).T.astype(BF16)
            for q in range(8):
                send_ref[q, pair, c * 16 : (c + 1) * 16, :] = turned[q * 16 : (q + 1) * 16]


ROOT = 0.7978845608028654


def first_grad_kernel(
    at_ref, mine_ref, other_ref, x_ref, back_ref, after_ref, gx_ref, keep_ref, send_ref
):
    first = at_ref[1] == 0
    row = lax.broadcasted_iota(jnp.int32, (128, 128), 0)
    col = lax.broadcasted_iota(jnp.int32, (128, 128), 1)
    pick = jnp.where(col == row % 32 * 4 + row // 32, 1.0, 0.0).astype(BF16)
    kept, sent = [], []
    for i in range(NB):
        mine, other = first_rows(mine_ref, i), first_rows(other_ref, i)
        zero, one = jnp.where(first, mine, other), jnp.where(first, other, mine)
        x = dot(pick, x_ref[:, i * 128 : (i + 1) * 128], 1, 1).astype(BF16)
        w = jnp.concatenate(
            [jnp.concatenate([zero[c], zero[4 + c], one[c], one[4 + c]]) for c in range(4)], axis=1
        ).astype(BF16)
        v = dot(w.T, x, 1, 0)
        square = v * v
        th = jnp.tanh(ROOT * (v + 0.044715 * (v * square)))
        slope = 0.5 * (1.0 + th) + (0.5 * ROOT) * v * (1.0 - th * th) * (1.0 + 0.134145 * square)
        back = jnp.concatenate([back_ref[:, i * 4 + c].reshape(128, ROWS) for c in range(4)])
        d = (back.astype(F32) * slope).astype(BF16)
        gx = dot(w, d, 1, 0)
        grad = dot(x, d, 1, 1).reshape(4, 32, 512)
        grads = [grad[:, :, c * 128 : (c + 1) * 128] for c in range(4)]
        gx_ref[:, i * 128 : (i + 1) * 128] = dot(gx.astype(BF16), pick, 0, 0).astype(BF16)
        by_core = [
            jnp.swapaxes(jnp.stack([grads[c][core * 2 + k] for k in range(2) for c in range(4)]), 0, 1)
            for core in range(2)
        ]
        kept.append(jnp.where(first, by_core[0], by_core[1]))
        sent.append(jnp.where(first, by_core[1], by_core[0]))
        if i % 2:
            rows = slice(i * 8 - 8, i * 8 + 8)
            keep_ref[:, rows, :] = jnp.concatenate(kept, axis=1).astype(BF16)
            send_ref[:, rows, :] = jnp.concatenate(sent, axis=1).astype(BF16)
            kept, sent = [], []


def second_grad_kernel(
    at_ref, x_ref, mine_ref, other_ref, c_ref, wmine_ref, wother_ref, out_ref, keep_ref,
    send_ref, mixed_ref, wide,
):
    first = at_ref[1] == 0
    row = lax.broadcasted_iota(jnp.int32, (256, 256), 0)
    col = lax.broadcasted_iota(jnp.int32, (256, 256), 1)
    target = (row // 64 % 2) * 128 + (row % 32) * 4 + (row // 128) * 2 + row // 32 % 2
    place = jnp.where(col == target, 1.0, 0.0).astype(BF16)
    for p in range(8):
        mine = mine_ref[p].reshape(192, 128).astype(F32)
        other = other_ref[p].reshape(192, 128).astype(F32)
        w = jnp.concatenate(
            [jnp.where(first, mine, other), jnp.where(first, other, mine)], axis=1
        ).astype(BF16)
        w = dot(w, place, 1, 0).astype(BF16)
        for i in range(NB):
            rows = slice(i // 2 * 64, i // 2 * 64 + 64)
            v = dot(
                w[rows, i % 2 * 128 : i % 2 * 128 + 128], x_ref[p, :, i * 128 : (i + 1) * 128], 1, 1
            )
            th = jnp.tanh(ROOT * (v + 0.044715 * (v * (v * v))))
            act = (0.5 * v) * (1.0 + th)
            start = (p * NB + i) * 4
            wide[start : start + 4] = act.reshape(4, 16, ROWS)
    for g in range(0, 192, 16):
        for n in range(2):
            cut = slice(n * 128, n * 128 + 128)
            part = jnp.swapaxes(wide[g : g + 16, :, cut], 0, 1).astype(BF16)
            for j in range(16):
                mixed_ref[j * 192 + g : j * 192 + g + 16, cut] = part[j]
    for pair in range(NB // 2):
        kept, sent = [], []
        wout = second_factor(first, wmine_ref, wother_ref, pair)
        for k in range(2):
            o = pair * 2 + k
            m = mixed_ref[o * 512 : (o + 1) * 512, :]
            out_ref[:, o * 128 : (o + 1) * 128] = dot(m, wout[k], 0, 0).astype(BF16)
            g = dot(m, c_ref[:, o * 128 : (o + 1) * 128], 1, 0).reshape(32, 2, 8, 128)
            kept.append(jnp.where(first, g[:, 0], g[:, 1]))
            sent.append(jnp.where(first, g[:, 1], g[:, 0]))
        rows = slice(pair * 16, pair * 16 + 16)
        keep_ref[:, rows, :] = jnp.concatenate(kept, axis=1).astype(BF16)
        send_ref[:, rows, :] = jnp.concatenate(sent, axis=1).astype(BF16)


def call(kernel, name, args, outs, scratch=(), unread=()):
    return pl.pallas_call(
        kernel,
        name=name,
        out_shape=[jax.ShapeDtypeStruct(shape, dtype) for shape, dtype in outs],
        in_specs=[
            ANY if n in unread else SMEM if arg.ndim == 1 else VMEM for n, arg in enumerate(args)
        ],
        out_specs=[VMEM] * len(outs),
        scratch_shapes=[pltpu.VMEM(shape, F32 if dtype is F32 else BF16) for shape, dtype in scratch],
        compiler_params=PARAMS,
        cost_estimate=pl.CostEstimate(
            flops=2 * 256 * 128 * 512 * 6, bytes_accessed=6_000_000, transcendentals=0
        ),
    )(*args)


def join_kernel(at_ref, keep_in, got_in, keep_out, got_out, both_ref):
    for n in range(32):
        place = lax.rem(n % RUN + RUN // 2 * at_ref[1], RUN)
        turn = RUNS // 2 * at_ref[1] + RUNS // 4 * (n % RUN)
        run = lax.rem((n % 16 // RUN - turn) * (1 - 2 * at_ref[1]) + 4 * RUNS, RUNS)
        to = lax.rem(n // 16 + at_ref[1], 2) * 16 + place * RUNS + run
        both_ref[to, :48, :] = (keep_in[n].astype(F32) + got_in[n].astype(F32)).astype(BF16)
        both_ref[to, 48:, :] = (keep_out[n].astype(F32) + got_out[n].astype(F32)).astype(BF16)


def part_kernel(got_ref, part_ref):
    total = got_ref[0].astype(F32)
    for n in range(1, 2 * RUN):
        total = total + got_ref[n].astype(F32)
    part_ref[...] = total.astype(BF16)


def total_kernel(got_ref, in_ref, out_ref):
    total = got_ref[0].astype(F32)
    for n in range(1, RUNS):
        total = total + got_ref[n].astype(F32)
    total = total * (1.0 / 128.0)
    out_ref[...] = total[48:].reshape(NB, 8, 128)
    for i in range(NB):
        for k in range(2):
            for c in range(4):
                row = i * 8 + k * 4 + c
                in_ref[i, k : k + 1, c * 128 : (c + 1) * 128] = total[row : row + 1]


RUN = 2
RUNS = 16 // RUN
NEAR = [
    [x * 32 + (run * RUN + RUN // 2 * core + n) % 16 * 2 + core for x in (core, 1 - core) for n in range(RUN)]
    for core in range(2)
    for run in range(RUNS)
]
FAR = [
    [
        x * 32 + ((run * (1 - 2 * core) + RUNS // 2 * core + RUNS // 4 * n) % RUNS * RUN + n) * 2 + core
        for run in range(RUNS)
    ]
    for x in range(2)
    for n in range(RUN)
    for core in range(2)
]


def exchange(value, axis, groups=None):
    return lax.all_to_all(value, axis, 0, 0, axis_index_groups=groups, tiled=True)


def swap_cores(value):
    return lax.ppermute(value, "core", [(0, 1), (1, 0)])


def on_device(tokens, w_in, w_out, cotangent):
    at = jnp.stack([lax.axis_index(MP), lax.axis_index("core")]).astype(jnp.int32)
    shard, copies = pl.pallas_call(
        start_kernel,
        name="start",
        out_shape=[
            jax.ShapeDtypeStruct((96, 128), BF16),
            jax.ShapeDtypeStruct((8, ROWS, 768), BF16),
        ],
        in_specs=[VMEM, VMEM, VMEM],
        out_specs=[VMEM, ANY],
        scratch_shapes=[pltpu.SemaphoreType.DMA((8,))],
        compiler_params=pltpu.CompilerParams(vmem_limit_bytes=62 * 1024 * 1024),
    )(w_in.transpose(1, 0, 2), w_out.transpose(1, 0, 2), tokens)
    pair = lax.all_gather(shard, "x_hi", axis=0, tiled=False)
    copies, pair = lax.optimization_barrier((copies, pair))
    gathered = exchange(copies, MP)
    mine = lax.all_gather(pair, "z", axis=0, tiled=False)
    other = swap_cores(mine)

    half = ((32, 48, 128), BF16)
    (column_send,) = call(
        columns_kernel, "columns", (mine,), [((8, 3, 64, 128), BF16)]
    )
    column_send, gathered = lax.optimization_barrier((column_send, gathered))
    columns = exchange(column_send, MP)
    other_columns = swap_cores(columns)
    (back_send,) = call(
        back_kernel, "d_mixed", (at, mine, other, cotangent),
        [((8, 24, 16, ROWS), BF16)], [((16, 192, ROWS), F32)],
    )
    back = exchange(back_send, MP)
    output, keep_out, send_out = call(
        second_grad_kernel, "second_grad",
        (at, gathered, columns, other_columns, cotangent, mine, other),
        [((ROWS, 768), BF16), half, half],
        [((3072, ROWS), BF16), ((192, 16, ROWS), F32)],
    )
    got_out = swap_cores(send_out)
    grad_tokens, keep_in, send_in = call(
        first_grad_kernel, "first_grad", (at, mine, other, tokens, back, got_out),
        [((ROWS, 768), BF16), half, half], (), (5,),
    )
    got_in = swap_cores(send_in)
    (both,) = call(
        join_kernel, "join", (at, keep_in, got_in, keep_out, got_out), [((32, 96, 128), BF16)]
    )
    near = exchange(both.reshape(2 * RUN, RUNS, 96, 128), DP, NEAR)
    (part,) = call(part_kernel, "part", (near,), [((RUNS, 96, 128), BF16)])
    grad_in, grad_out = call(
        total_kernel, "total", (exchange(part, DP, FAR),),
        [((NB, 2, 512), F32), ((NB, 8, 128), F32)],
    )
    grad_in, grad_out = grad_in.transpose(1, 0, 2), grad_out.transpose(1, 0, 2)
    return (output, grad_tokens, grad_in, grad_out)


def solution(mesh):
    fine = Mesh(mesh.devices.reshape(SIZES), DP + MP)
    placed = (P(DP, MP), P(DP, MP, None), P(DP, MP, None), P(DP, MP))
    return jax.shard_map(
        on_device,
        mesh=fine,
        in_specs=placed,
        out_specs=(P(DP, MP), P(DP, MP), P(DP, MP, None), P(DP, MP, None)),
        check_vma=False,
    )
```

```python
import jax
import jax.numpy as jnp
from jax import lax
from jax.experimental import pallas as pl
from jax.experimental.pallas import tpu as pltpu
from jax.sharding import Mesh, PartitionSpec as P

NB = 6
ROWS = 256
DP = ("x_hi", "z", "core")
MP = ("x_lo", "y")
SIZES = (2, 16, 2, 2, 4)
F32 = jnp.float32
BF16 = jnp.bfloat16
PARAMS = pltpu.CompilerParams(vmem_limit_bytes=20 * 1024 * 1024)
SMEM = pl.BlockSpec(memory_space=pltpu.SMEM)
ANY = pl.BlockSpec(memory_space=pl.ANY)
VMEM = pl.BlockSpec(memory_space=pltpu.VMEM)


def dot(lhs, rhs, lhs_dim, rhs_dim):
    return lax.dot_general(
        lhs, rhs, (((lhs_dim,), (rhs_dim,)), ((), ())), preferred_element_type=F32
    )


def halves(value, step):
    return value[:, step * 128 : (step + 1) * 128]


def start_kernel(win_ref, wout_ref, x_ref, shard_ref, copies_ref, sems):
    copies = [pltpu.make_async_copy(x_ref, copies_ref.at[q], sems.at[q]) for q in range(8)]
    for copy in copies:
        copy.start()
    rows = []
    for i in range(NB):
        w = win_ref[i].astype(F32)
        rows += [w[k : k + 1, c * 128 : (c + 1) * 128] for k in range(2) for c in range(4)]
    shard_ref[:48, :] = jnp.concatenate(rows).astype(BF16)
    shard_ref[48:, :] = wout_ref[...].astype(F32).reshape(48, 128).astype(BF16)
    for copy in copies:
        copy.wait()


def shard_rows(ref, rows):
    return jnp.concatenate([ref[:, 0, rows], ref[:, 1, rows]], axis=0).astype(F32)


def second_factor(first, mine_ref, other_ref, pair):
    rows = slice(48 + pair * 16, 48 + pair * 16 + 16)
    mine, other = shard_rows(mine_ref, rows), shard_rows(other_ref, rows)
    zero = jnp.where(first, mine, other)
    one = jnp.where(first, other, mine)
    return [
        jnp.stack([zero[:, cut], one[:, cut]], axis=1).reshape(512, 128).astype(BF16)
        for cut in (slice(0, 8), slice(8, 16))
    ]


def back_kernel(at_ref, mine_ref, other_ref, c_ref, send_ref, wide):
    first = at_ref[1] == 0
    for pair in range(NB // 2):
        for k, w in enumerate(second_factor(first, mine_ref, other_ref, pair)):
            o = pair * 2 + k
            d = dot(w, c_ref[:, o * 128 : (o + 1) * 128], 1, 1).reshape(8, 64, ROWS)
            for n in range(8):
                at = o * 512 + n * 64
                wide[at // 192, at % 192 : at % 192 + 64, :] = d[n]
    for p in range(8):
        for n in range(2):
            cut = slice(n * 128, n * 128 + 128)
            part = jnp.swapaxes(wide[:, p * 24 : (p + 1) * 24, cut], 0, 1)
            send_ref[lax.rem(p + 4 * at_ref[1], 8), :, :, cut] = part.astype(BF16)


def first_rows(ref, i):
    both = shard_rows(ref, slice(i // 2 * 16, i // 2 * 16 + 16))
    return jnp.swapaxes(both[:, i % 2 * 8 : i % 2 * 8 + 8], 0, 1)


def columns_kernel(at_ref, mine_ref, send_ref):
    for pair in range(NB // 2):
        blocks = [first_rows(mine_ref, pair * 2), first_rows(mine_ref, pair * 2 + 1)]
        for c in range(4):
            rows = [blocks[i][k * 4 + c] for i in range(2) for k in range(2)]
            turned = jnp.concatenate(rows, axis=0).T.astype(BF16)
            for q in range(8):
                to = lax.rem(q + 4 * at_ref[1], 8)
                send_ref[to, pair, c * 16 : (c + 1) * 16, :] = turned[q * 16 : (q + 1) * 16]


ROOT = 0.7978845608028654


def first_grad_kernel(
    at_ref, mine_ref, other_ref, x_ref, back_ref, after_ref, gx_ref, keep_ref, send_ref
):
    first = at_ref[1] == 0
    row = lax.broadcasted_iota(jnp.int32, (128, 128), 0)
    col = lax.broadcasted_iota(jnp.int32, (128, 128), 1)
    pick = jnp.where(col == row % 32 * 4 + row // 32, 1.0, 0.0).astype(BF16)
    kept, sent = [], []
    for i in range(NB):
        mine, other = first_rows(mine_ref, i), first_rows(other_ref, i)
        zero, one = jnp.where(first, mine, other), jnp.where(first, other, mine)
        x = dot(pick, x_ref[:, i * 128 : (i + 1) * 128], 1, 1).astype(BF16)
        w = jnp.concatenate(
            [jnp.concatenate([zero[c], zero[4 + c], one[c], one[4 + c]]) for c in range(4)], axis=1
        ).astype(BF16)
        v = dot(w.T, x, 1, 0)
        square = v * v
        th = jnp.tanh(ROOT * (v + 0.044715 * (v * square)))
        slope = 0.5 * (1.0 + th) + (0.5 * ROOT) * v * (1.0 - th * th) * (1.0 + 0.134145 * square)
        low, high = pl.ds(4 * at_ref[1], 4), pl.ds(4 - 4 * at_ref[1], 4)
        back = jnp.concatenate(
            [back_ref[half, i * 4 + c].reshape(64, ROWS) for c in range(4) for half in (low, high)]
        )
        d = (back.astype(F32) * slope).astype(BF16)
        gx = dot(w, d, 1, 0)
        grad = dot(x, d, 1, 1).reshape(4, 32, 512)
        grads = [grad[:, :, c * 128 : (c + 1) * 128] for c in range(4)]
        gx_ref[:, i * 128 : (i + 1) * 128] = dot(gx.astype(BF16), pick, 0, 0).astype(BF16)
        by_core = [
            jnp.swapaxes(jnp.stack([grads[c][core * 2 + k] for k in range(2) for c in range(4)]), 0, 1)
            for core in range(2)
        ]
        kept.append(jnp.where(first, by_core[0], by_core[1]))
        sent.append(jnp.where(first, by_core[1], by_core[0]))
        if i % 2:
            rows = slice(i * 8 - 8, i * 8 + 8)
            keep_ref[:, rows, :] = jnp.concatenate(kept, axis=1).astype(BF16)
            send_ref[:, rows, :] = jnp.concatenate(sent, axis=1).astype(BF16)
            kept, sent = [], []


def second_grad_kernel(
    at_ref, x_ref, mine_ref, other_ref, c_ref, wmine_ref, wother_ref, out_ref, keep_ref,
    send_ref, mixed_ref, wide,
):
    first = at_ref[1] == 0
    row = lax.broadcasted_iota(jnp.int32, (256, 256), 0)
    col = lax.broadcasted_iota(jnp.int32, (256, 256), 1)
    target = (row // 64 % 2) * 128 + (row % 32) * 4 + (row // 128) * 2 + row // 32 % 2
    place = jnp.where(col == target, 1.0, 0.0).astype(BF16)
    for s in range(8):
        p = lax.rem(s + 4 * at_ref[1], 8)
        mine = mine_ref[s].reshape(192, 128).astype(F32)
        other = other_ref[(s + 4) % 8].reshape(192, 128).astype(F32)
        w = jnp.concatenate(
            [jnp.where(first, mine, other), jnp.where(first, other, mine)], axis=1
        ).astype(BF16)
        w = dot(w, place, 1, 0).astype(BF16)
        for i in range(NB):
            rows = slice(i // 2 * 64, i // 2 * 64 + 64)
            v = dot(
                w[rows, i % 2 * 128 : i % 2 * 128 + 128], x_ref[s, :, i * 128 : (i + 1) * 128], 1, 1
            )
            th = jnp.tanh(ROOT * (v + 0.044715 * (v * (v * v))))
            act = (0.5 * v) * (1.0 + th)
            start = (p * NB + i) * 4
            wide[pl.ds(start, 4)] = act.reshape(4, 16, ROWS)
    for g in range(0, 192, 16):
        for n in range(2):
            cut = slice(n * 128, n * 128 + 128)
            part = jnp.swapaxes(wide[g : g + 16, :, cut], 0, 1).astype(BF16)
            for j in range(16):
                mixed_ref[j * 192 + g : j * 192 + g + 16, cut] = part[j]
    for pair in range(NB // 2):
        kept, sent = [], []
        wout = second_factor(first, wmine_ref, wother_ref, pair)
        for k in range(2):
            o = pair * 2 + k
            m = mixed_ref[o * 512 : (o + 1) * 512, :]
            out_ref[:, o * 128 : (o + 1) * 128] = dot(m, wout[k], 0, 0).astype(BF16)
            g = dot(m, c_ref[:, o * 128 : (o + 1) * 128], 1, 0).reshape(32, 2, 8, 128)
            kept.append(jnp.where(first, g[:, 0], g[:, 1]))
            sent.append(jnp.where(first, g[:, 1], g[:, 0]))
        rows = slice(pair * 16, pair * 16 + 16)
        keep_ref[:, rows, :] = jnp.concatenate(kept, axis=1).astype(BF16)
        send_ref[:, rows, :] = jnp.concatenate(sent, axis=1).astype(BF16)


def call(kernel, name, args, outs, scratch=(), unread=()):
    return pl.pallas_call(
        kernel,
        name=name,
        out_shape=[jax.ShapeDtypeStruct(shape, dtype) for shape, dtype in outs],
        in_specs=[
            ANY if n in unread else SMEM if arg.ndim == 1 else VMEM for n, arg in enumerate(args)
        ],
        out_specs=[VMEM] * len(outs),
        scratch_shapes=[pltpu.VMEM(shape, F32 if dtype is F32 else BF16) for shape, dtype in scratch],
        compiler_params=PARAMS,
        cost_estimate=pl.CostEstimate(
            flops=2 * 256 * 128 * 512 * 6, bytes_accessed=6_000_000, transcendentals=0
        ),
    )(*args)


def join_kernel(at_ref, keep_in, got_in, keep_out, got_out, both_ref):
    for n in range(32):
        place = lax.rem(n % RUN + RUN // 2 * at_ref[1], RUN)
        turn = RUNS // 2 * at_ref[1] + RUNS // 4 * (n % RUN)
        run = lax.rem((n % 16 // RUN - turn) * (1 - 2 * at_ref[1]) + 4 * RUNS, RUNS)
        to = lax.rem(n // 16 + at_ref[1], 2) * 16 + place * RUNS + run
        both_ref[to, :48, :] = (keep_in[n].astype(F32) + got_in[n].astype(F32)).astype(BF16)
        both_ref[to, 48:, :] = (keep_out[n].astype(F32) + got_out[n].astype(F32)).astype(BF16)


def part_kernel(got_ref, part_ref):
    total = got_ref[0].astype(F32)
    for n in range(1, 2 * RUN):
        total = total + got_ref[n].astype(F32)
    part_ref[...] = total.astype(BF16)


def total_kernel(got_ref, in_ref, out_ref):
    total = got_ref[0].astype(F32)
    for n in range(1, RUNS):
        total = total + got_ref[n].astype(F32)
    total = total * (1.0 / 128.0)
    out_ref[...] = total[48:].reshape(NB, 8, 128)
    for i in range(NB):
        for k in range(2):
            for c in range(4):
                row = i * 8 + k * 4 + c
                in_ref[i, k : k + 1, c * 128 : (c + 1) * 128] = total[row : row + 1]


RUN = 2
RUNS = 16 // RUN
NEAR = [
    [x * 32 + (run * RUN + RUN // 2 * core + n) % 16 * 2 + core for x in (core, 1 - core) for n in range(RUN)]
    for core in range(2)
    for run in range(RUNS)
]
FAR = [
    [
        x * 32 + ((run * (1 - 2 * core) + RUNS // 2 * core + RUNS // 4 * n) % RUNS * RUN + n) * 2 + core
        for run in range(RUNS)
    ]
    for x in range(2)
    for n in range(RUN)
    for core in range(2)
]


ACROSS = ("core", "x_lo", "y")
BLOCKS = [[core * 8 + (n + 4 * core) % 8 for n in range(8)] for core in range(2)]


def exchange(value, axis, groups=None):
    return lax.all_to_all(value, axis, 0, 0, axis_index_groups=groups, tiled=True)


def swap_cores(value):
    return lax.ppermute(value, "core", [(0, 1), (1, 0)])


def on_device(tokens, w_in, w_out, cotangent):
    at = jnp.stack([lax.axis_index(MP), lax.axis_index("core")]).astype(jnp.int32)
    shard, copies = pl.pallas_call(
        start_kernel,
        name="start",
        out_shape=[
            jax.ShapeDtypeStruct((96, 128), BF16),
            jax.ShapeDtypeStruct((8, ROWS, 768), BF16),
        ],
        in_specs=[VMEM, VMEM, VMEM],
        out_specs=[VMEM, ANY],
        scratch_shapes=[pltpu.SemaphoreType.DMA((8,))],
        compiler_params=pltpu.CompilerParams(vmem_limit_bytes=62 * 1024 * 1024),
    )(w_in.transpose(1, 0, 2), w_out.transpose(1, 0, 2), tokens)
    pair = lax.all_gather(shard, "x_hi", axis=0, tiled=False)
    copies, pair = lax.optimization_barrier((copies, pair))
    gathered = exchange(copies, ACROSS, BLOCKS)
    mine = lax.all_gather(pair, "z", axis=0, tiled=False)
    other = swap_cores(mine)

    half = ((32, 48, 128), BF16)
    (column_send,) = call(
        columns_kernel, "columns", (at, mine), [((8, 3, 64, 128), BF16)]
    )
    column_send, gathered = lax.optimization_barrier((column_send, gathered))
    columns = exchange(column_send, ACROSS, BLOCKS)
    other_columns = swap_cores(columns)
    (back_send,) = call(
        back_kernel, "d_mixed", (at, mine, other, cotangent),
        [((8, 24, 16, ROWS), BF16)], [((16, 192, ROWS), F32)],
    )
    back = exchange(back_send, ACROSS, BLOCKS)
    output, keep_out, send_out = call(
        second_grad_kernel, "second_grad",
        (at, gathered, columns, other_columns, cotangent, mine, other),
        [((ROWS, 768), BF16), half, half],
        [((3072, ROWS), BF16), ((192, 16, ROWS), F32)],
    )
    got_out = swap_cores(send_out)
    grad_tokens, keep_in, send_in = call(
        first_grad_kernel, "first_grad", (at, mine, other, tokens, back, got_out),
        [((ROWS, 768), BF16), half, half], (), (5,),
    )
    got_in = swap_cores(send_in)
    (both,) = call(
        join_kernel, "join", (at, keep_in, got_in, keep_out, got_out), [((32, 96, 128), BF16)]
    )
    near = exchange(both.reshape(2 * RUN, RUNS, 96, 128), DP, NEAR)
    (part,) = call(part_kernel, "part", (near,), [((RUNS, 96, 128), BF16)])
    grad_in, grad_out = call(
        total_kernel, "total", (exchange(part, DP, FAR),),
        [((NB, 2, 512), F32), ((NB, 8, 128), F32)],
    )
    grad_in, grad_out = grad_in.transpose(1, 0, 2), grad_out.transpose(1, 0, 2)
    return (output, grad_tokens, grad_in, grad_out)


def solution(mesh):
    fine = Mesh(mesh.devices.reshape(SIZES), DP + MP)
    placed = (P(DP, MP), P(DP, MP, None), P(DP, MP, None), P(DP, MP))
    return jax.shard_map(
        on_device,
        mesh=fine,
        in_specs=placed,
        out_specs=(P(DP, MP), P(DP, MP), P(DP, MP, None), P(DP, MP, None)),
        check_vma=False,
    )
```
